128 devices in a mesh: row: 8 (over y, core), grp: 16 (over x, z).
Axes of the slice: x: 4, y: 4, z: 4, core: 2. Of those that a mesh axis runs over, the one named last changes fastest.
Arguments:
- embeddings: bfloat16 [57344, 1024], P(('row', 'grp')), may hold values from -16 to 16
- scales: float32 [57344, 8], P(('row', 'grp')), may hold values from 0.3 to 3
- cluster_id: int32 [57344], P(('row', 'grp')), may hold values from 0 to 7, as said below
- doc_rank: int32 [57344], P(('row', 'grp')), may hold values from 0 to 14335, as said below
Outputs:
- nearest: float32 [57344], P(('row', 'grp'))
The draws below stay inside these ranges and needn't reach their ends.
Inputs may be any that keep to these rules, and one draw needn't show every extreme that they name: `cluster_id`: within each cluster the doc_rank values are 0, 1, and so on up to the cluster's size less one, each once; some cluster has exactly 14336 documents. `doc_rank`: counting a document of cluster c and rank k toward slot group c * 16 + (k mod 16), each aligned block of 448 documents holds at most 7 documents of any one slot group, and in every draw some slot group has exactly 7 documents in every block.
All inputs are finite; a program needn't handle non-finite values.
Results may differ from the reference program's by a relative error of at most 0.00068.
Values may be sent and summed in bfloat16 or wider, within the bound.
A program may use at most 128 MiB of HBM per device.

```python
import math
import jax
import jax.numpy as jnp
from jax import lax

D = 1024
SCALES = 8
DOC_DEV = 448
SLOTS = 896
CAP = 14336
CLUSTERS = 8
DOCS = 57344


def arrangement(key):
    devices = DOCS // DOC_DEV
    slot_total = CLUSTERS * CAP
    key_full, key_rate, key_mix, key_pos, key_family = jax.random.split(key, 5)
    full_cluster = jax.random.randint(key_full, (), 0, CLUSTERS)
    fill_rate = jax.random.randint(key_rate, (CLUSTERS,), 1, 9)
    slot_ids = jnp.arange(slot_total, dtype=jnp.int32)
    owner_of = slot_ids // CAP
    order_in = slot_ids % CAP
    priority = order_in * fill_rate[owner_of] + CAP
    priority = jnp.where(owner_of == full_cluster, order_in, priority)
    priority = priority * CLUSTERS + owner_of
    chosen = jnp.argsort(priority, stable=True)[:DOCS].astype(jnp.int32)
    cluster_of = chosen // CAP
    rank_of = chosen % CAP
    group_size = CAP // SLOTS
    slot_group = cluster_of * group_size + rank_of % group_size
    shuffle_order = jax.random.permutation(key_mix, DOCS).astype(jnp.int32)
    sequence = shuffle_order[jnp.argsort(slot_group[shuffle_order], stable=True)]
    arrival = jnp.arange(DOCS, dtype=jnp.int32)
    source = arrival % devices
    local_place = arrival // devices
    shuffles = jax.vmap(lambda sub_key: jax.random.permutation(sub_key, DOC_DEV))(jax.random.split(key_pos, devices)).astype(jnp.int32)
    target = source * DOC_DEV + shuffles[source, local_place]
    cluster_id = jnp.zeros((DOCS,), jnp.int32).at[target].set(cluster_of[sequence])
    doc_rank = jnp.zeros((DOCS,), jnp.int32).at[target].set(rank_of[sequence])
    family_slot = jax.random.randint(key_family, (slot_total,), 0, max(1, CAP // 8))
    family = jnp.zeros((DOCS,), jnp.int32).at[target].set(family_slot[chosen[sequence]])
    return (cluster_id, doc_rank, family)


def draw_cluster_id(key, part):
    shared = arrangement(key)
    return shared[0]


def draw_doc_rank(key, part):
    shared = arrangement(key)
    return shared[1]


def draw_embeddings(key, part):
    shared = arrangement(key)
    key = jax.random.fold_in(key, 3)
    cluster_id = shared[0]
    family = shared[2]
    families = max(1, CAP // 8)
    key_chan, key_cent, key_fam, key_noise, key_weight = jax.random.split(key, 5)
    channel_scale = jnp.exp(jax.random.uniform(key_chan, (D,), minval=jnp.log(0.3), maxval=jnp.log(3.0)))
    centroid = jax.random.normal(key_cent, (CLUSTERS, D))[cluster_id]
    family_vec = jax.random.normal(key_fam, (CLUSTERS * families, D))[cluster_id * families + family]
    weight = jax.random.uniform(key_weight, (DOCS, 1), minval=0.3, maxval=2.5)
    noise_part = jax.random.normal(key_noise, (DOCS, D))
    mixed = 0.5 * centroid + weight * family_vec + noise_part
    return jnp.clip(mixed * channel_scale[None, :], -16.0, 16.0).astype(jnp.bfloat16)


def level_of(stream_key, extent, cuts, least, high):
    def one(dim, parts):
        heights = jax.random.uniform(jax.random.fold_in(jax.random.fold_in(stream_key, 6), dim), (parts,), jnp.float32, least / len(cuts), high / len(cuts))
        return jnp.repeat(jnp.exp(heights), extent[dim] // parts).reshape((-1,) + (1,) * (len(extent) - dim - 1))

    loudness = one(*cuts[0])
    for cut in cuts[1:]:
        loudness = loudness * one(*cut)
    return loudness


def setup_inputs(seed: int = 0) -> dict:
    keys = jax.random.split(jax.random.key(seed), 5)
    embeddings = draw_embeddings(jax.random.fold_in(keys[4], 71), 0)
    scales = jnp.clip(jnp.exp(math.log(3.0) - 2.3025851 * jax.random.uniform(keys[1], (DOCS, SCALES), jnp.float32) ** level_of(keys[1], (DOCS, SCALES), ((0, 128),), -0.2, 0.2)), 0.3, 3.0)
    cluster_id = draw_cluster_id(jax.random.fold_in(keys[4], 71), 0)
    doc_rank = draw_doc_rank(jax.random.fold_in(keys[4], 71), 0)
    return {"embeddings": embeddings, "scales": scales, "cluster_id": cluster_id, "doc_rank": doc_rank}


def unit_rows(embeddings, scales):
    doc_count, feature_dim = embeddings.shape
    blocks = scales.shape[1]
    scaled = (embeddings.astype(jnp.float32).reshape(doc_count, blocks, feature_dim // blocks) * scales[:, :, None]).reshape(doc_count, feature_dim)
    squares = lax.optimization_barrier(jnp.sum(scaled * scaled, axis=1, keepdims=True))
    return (scaled * lax.rsqrt(squares + 1e-06)).astype(jnp.bfloat16)

def reference(embeddings, scales, cluster_id, doc_rank):
    unit_vecs = unit_rows(embeddings, scales)
    slot_of = (cluster_id * CAP + doc_rank).astype(jnp.int32)
    slot_table = jnp.zeros((CLUSTERS * CAP, D), jnp.bfloat16).at[slot_of].set(unit_vecs)
    slot_table = slot_table.reshape(CLUSTERS, CAP, D)
    slot_ranks = jnp.arange(CAP, dtype=jnp.int32)
    block_rows = math.gcd(CAP, 512)

    def per_cluster(members):
        as_float = members.astype(jnp.float32)

        def per_block(block_id):
            row_block = lax.dynamic_slice_in_dim(as_float, block_id * block_rows, block_rows, 0)
            scores = lax.dot_general(row_block, as_float, (((1,), (1,)), ((), ())), precision=lax.Precision.HIGHEST, preferred_element_type=jnp.float32)
            own_ranks = block_id * block_rows + jnp.arange(block_rows, dtype=jnp.int32)
            masked = jnp.where(slot_ranks[None, :] < own_ranks[:, None], scores, -1.0)
            return lax.optimization_barrier(jnp.max(masked, axis=1))
        return lax.map(per_block, jnp.arange(CAP // block_rows, dtype=jnp.int32)).reshape(CAP)
    best_sim = lax.map(per_cluster, slot_table)
    return best_sim.reshape(CLUSTERS * CAP)[slot_of]
```

```python
import functools

import jax
import jax.numpy as jnp
from jax import lax
from jax.experimental import pallas as pl
from jax.experimental.pallas import tpu as pltpu
from jax.sharding import PartitionSpec as P

MESH = pl.DeviceIdType.MESH

OFFSETS = (
    (0, 0, 0), (3, 0, 0), (0, 1, 0), (1, 0, 0), (0, 0, 1), (1, 0, 3), (0, 2, 0), (3, 2, 0), (0, 0, 2), (1, 0, 2),
    (3, 3, 0), (1, 3, 3),
)
SLOTS = len(OFFSETS)
CHUNKS = 7
SORT, ARRIVE, SEND, BEGIN, READY, PAIRS, SHARED, OWN = range(8)
PLAN = (
    (SORT, 0), (SORT, 1), (ARRIVE, 0, 0, 0), (ARRIVE, 1, 0, 0), (SEND, 0, 0, 3, 0), (SEND, 0, 0, 1, 0),
    (SEND, 0, 0, 2, 0), (SEND, 0, 0, 4, 0), (SORT, 2), (ARRIVE, 0, 0, 1), (ARRIVE, 1, 0, 1), (SEND, 1, 0, 3, 0),
    (SEND, 1, 0, 1, 0), (SEND, 1, 0, 2, 0), (SEND, 1, 0, 4, 0), (SORT, 3), (ARRIVE, 0, 0, 2), (ARRIVE, 1, 0, 2),
    (SORT, 4), (ARRIVE, 0, 0, 3), (ARRIVE, 1, 0, 3), (SORT, 5), (ARRIVE, 0, 0, 4), (ARRIVE, 1, 0, 4), (SORT, 6),
    (ARRIVE, 0, 0, 5), (ARRIVE, 1, 0, 5), (ARRIVE, 0, 0, 6), (ARRIVE, 1, 0, 6), (SEND, 0, 0, 3, 1),
    (SEND, 0, 0, 1, 1), (SEND, 0, 0, 2, 1), (SEND, 0, 0, 4, 1), (BEGIN, 0), (READY, 0), (OWN,), (SEND, 1, 0, 3, 1),
    (SEND, 1, 0, 1, 1), (SEND, 1, 0, 2, 1), (SEND, 1, 0, 4, 1), (ARRIVE, 0, 3, 0), (ARRIVE, 0, 1, 0),
    (ARRIVE, 0, 2, 0), (ARRIVE, 0, 4, 0), (SEND, 0, 3, 5, 0), (SEND, 0, 1, 10, 0), (SEND, 0, 0, 3, 2),
    (SEND, 0, 0, 1, 2), (SEND, 0, 0, 2, 2), (SEND, 0, 0, 4, 2), (ARRIVE, 1, 3, 0), (ARRIVE, 1, 1, 0),
    (ARRIVE, 1, 2, 0), (ARRIVE, 1, 4, 0), (SEND, 1, 3, 5, 0), (SEND, 1, 1, 10, 0), (SEND, 1, 0, 3, 2),
    (SEND, 1, 0, 1, 2), (SEND, 1, 0, 2, 2), (SEND, 1, 0, 4, 2), (BEGIN, 1), (BEGIN, 2), (BEGIN, 3), (BEGIN, 4),
    (ARRIVE, 0, 3, 1), (ARRIVE, 0, 1, 1), (ARRIVE, 0, 2, 1), (ARRIVE, 0, 4, 1), (SEND, 0, 3, 5, 1),
    (SEND, 0, 1, 10, 1), (SEND, 0, 0, 3, 3), (SEND, 0, 0, 1, 3), (SEND, 0, 0, 2, 3), (SEND, 0, 0, 4, 3),
    (ARRIVE, 1, 3, 1), (ARRIVE, 1, 1, 1), (ARRIVE, 1, 2, 1), (ARRIVE, 1, 4, 1), (SEND, 1, 3, 5, 1),
    (SEND, 1, 1, 10, 1), (ARRIVE, 0, 5, 0), (ARRIVE, 0, 10, 0), (SEND, 1, 0, 3, 3), (SEND, 1, 0, 1, 3),
    (SEND, 1, 0, 2, 3), (SEND, 1, 0, 4, 3), (SEND, 0, 10, 7, 0), (ARRIVE, 0, 3, 2), (ARRIVE, 0, 1, 2),
    (ARRIVE, 0, 2, 2), (ARRIVE, 0, 4, 2), (SEND, 0, 3, 5, 2), (ARRIVE, 1, 5, 0), (ARRIVE, 1, 10, 0),
    (SEND, 0, 0, 4, 4), (SEND, 1, 0, 3, 4), (SEND, 1, 0, 1, 4), (SEND, 1, 0, 2, 4), (SEND, 1, 10, 7, 0), (BEGIN, 5),
    (BEGIN, 10), (ARRIVE, 1, 3, 2), (ARRIVE, 1, 1, 2), (ARRIVE, 1, 2, 2), (ARRIVE, 1, 4, 2), (SEND, 1, 3, 5, 2),
    (ARRIVE, 0, 5, 1), (ARRIVE, 0, 10, 1), (SEND, 0, 0, 3, 4), (SEND, 0, 0, 1, 4), (SEND, 0, 0, 2, 4),
    (SEND, 1, 0, 4, 4), (SEND, 1, 5, 9, 0), (SEND, 0, 10, 7, 1), (ARRIVE, 0, 3, 3), (ARRIVE, 0, 1, 3),
    (ARRIVE, 0, 2, 3), (ARRIVE, 0, 4, 3), (ARRIVE, 1, 5, 1), (ARRIVE, 1, 10, 1), (SEND, 0, 4, 8, 0),
    (SEND, 1, 0, 3, 5), (SEND, 1, 0, 1, 5), (SEND, 1, 0, 2, 5), (SEND, 1, 10, 7, 1), (SEND, 0, 3, 5, 3),
    (ARRIVE, 1, 3, 3), (ARRIVE, 1, 1, 3), (ARRIVE, 1, 2, 3), (ARRIVE, 1, 4, 3), (ARRIVE, 0, 7, 0), (ARRIVE, 0, 5, 2),
    (SEND, 1, 4, 8, 0), (SEND, 0, 0, 3, 5), (SEND, 0, 0, 1, 5), (SEND, 0, 0, 2, 5), (SEND, 0, 1, 10, 2),
    (SEND, 1, 3, 5, 3), (ARRIVE, 0, 4, 4), (ARRIVE, 1, 3, 4), (ARRIVE, 1, 1, 4), (ARRIVE, 1, 2, 4),
    (ARRIVE, 1, 7, 0), (ARRIVE, 1, 5, 2), (SEND, 0, 7, 6, 0), (SEND, 1, 0, 4, 5), (SEND, 1, 0, 1, 6),
    (SEND, 1, 0, 2, 6), (SEND, 1, 5, 11, 0), (SEND, 0, 5, 9, 1), (BEGIN, 7), (ARRIVE, 0, 3, 4), (ARRIVE, 0, 1, 4),
    (ARRIVE, 0, 2, 4), (ARRIVE, 1, 4, 4), (ARRIVE, 1, 9, 0), (ARRIVE, 0, 7, 1), (SEND, 1, 7, 6, 0),
    (SEND, 0, 0, 4, 5), (SEND, 0, 0, 1, 6), (SEND, 0, 0, 2, 6), (SEND, 1, 3, 5, 4), (ARRIVE, 0, 8, 0),
    (ARRIVE, 1, 3, 5), (ARRIVE, 1, 1, 5), (ARRIVE, 1, 2, 5), (SEND, 1, 1, 10, 5), (ARRIVE, 1, 7, 1),
    (ARRIVE, 0, 5, 3), (SEND, 0, 8, 9, 0), (SEND, 0, 4, 8, 1), (SEND, 1, 2, 6, 2), (SEND, 0, 3, 5, 4),
    (ARRIVE, 1, 8, 0), (ARRIVE, 0, 3, 5), (ARRIVE, 0, 1, 5), (ARRIVE, 0, 2, 5), (SEND, 0, 1, 10, 5),
    (ARRIVE, 0, 10, 2), (ARRIVE, 1, 5, 3), (SEND, 1, 4, 8, 1), (SEND, 0, 2, 6, 3), (SEND, 1, 0, 3, 6),
    (SEND, 0, 5, 9, 2), (SEND, 0, 10, 7, 2), (BEGIN, 8), (ARRIVE, 0, 6, 0), (ARRIVE, 1, 4, 5), (ARRIVE, 1, 1, 6),
    (ARRIVE, 1, 2, 6), (ARRIVE, 1, 11, 0), (ARRIVE, 0, 9, 1), (SEND, 1, 2, 6, 3), (SEND, 0, 0, 3, 6),
    (SEND, 1, 0, 4, 6), (SEND, 0, 5, 11, 0), (SEND, 1, 3, 5, 5), (ARRIVE, 1, 6, 0), (ARRIVE, 0, 4, 5),
    (ARRIVE, 0, 1, 6), (ARRIVE, 0, 2, 6), (ARRIVE, 1, 5, 4), (ARRIVE, 1, 10, 5), (SEND, 1, 7, 6, 1),
    (SEND, 0, 2, 6, 4), (SEND, 0, 0, 4, 6), (SEND, 0, 3, 5, 5), (SEND, 1, 10, 7, 5), (BEGIN, 6), (READY, 1),
    (READY, 2), (ARRIVE, 0, 9, 0), (ARRIVE, 0, 8, 1), (ARRIVE, 1, 6, 2), (SEND, 1, 6, 7, 2), (ARRIVE, 0, 5, 4),
    (ARRIVE, 0, 10, 5), (PAIRS, 2, (0, 1)), (SEND, 0, 7, 6, 1), (SEND, 0, 4, 8, 2), (SEND, 1, 2, 6, 4),
    (SEND, 0, 10, 7, 5), (BEGIN, 9), (ARRIVE, 1, 8, 1), (ARRIVE, 0, 6, 3), (ARRIVE, 1, 3, 6), (SEND, 0, 6, 7, 3),
    (SEND, 1, 3, 5, 6), (ARRIVE, 0, 9, 2), (ARRIVE, 0, 7, 2), (SEND, 1, 8, 9, 1), (SEND, 1, 4, 8, 2),
    (SEND, 0, 2, 6, 6), (SEND, 0, 5, 11, 1), (ARRIVE, 1, 6, 3), (ARRIVE, 0, 3, 6), (ARRIVE, 1, 4, 6),
    (SEND, 1, 6, 7, 3), (SEND, 0, 3, 5, 6), (ARRIVE, 0, 11, 0), (ARRIVE, 1, 5, 5), (PAIRS, 1, (0,)),
    (SEND, 0, 7, 6, 2), (SEND, 0, 4, 8, 3), (SEND, 1, 2, 6, 6), (SEND, 1, 5, 11, 1), (SEND, 0, 5, 9, 4), (BEGIN, 11),
    (READY, 3), (ARRIVE, 1, 6, 1), (ARRIVE, 0, 6, 4), (ARRIVE, 0, 4, 6), (SEND, 0, 6, 7, 4), (ARRIVE, 1, 7, 2),
    (ARRIVE, 0, 5, 5), (ARRIVE, 1, 7, 5), (SEND, 1, 7, 10, 2), (SEND, 1, 4, 8, 3), (SEND, 1, 7, 6, 5),
    (SEND, 0, 5, 11, 2), (SEND, 1, 5, 9, 5), (PAIRS, 3, (2,)), (READY, 4), (ARRIVE, 0, 6, 1), (ARRIVE, 0, 8, 2),
    (ARRIVE, 1, 6, 4), (SEND, 1, 6, 7, 4), (ARRIVE, 0, 7, 3), (ARRIVE, 0, 7, 5), (ARRIVE, 1, 5, 6),
    (SEND, 0, 7, 10, 3), (SEND, 1, 4, 8, 4), (SEND, 0, 7, 6, 5), (SEND, 1, 5, 11, 2), (SEND, 0, 5, 9, 5),
    (PAIRS, 4, (0, 1, 2)), (ARRIVE, 1, 9, 1), (ARRIVE, 1, 8, 2), (ARRIVE, 0, 6, 6), (SEND, 0, 6, 7, 6),
    (ARRIVE, 0, 11, 1), (ARRIVE, 1, 7, 3), (ARRIVE, 0, 5, 6), (SEND, 1, 8, 9, 2), (SEND, 1, 7, 10, 3),
    (SEND, 0, 4, 8, 5), (SEND, 1, 5, 11, 3), (SEND, 1, 5, 9, 6), (ARRIVE, 0, 6, 2), (ARRIVE, 0, 8, 3),
    (ARRIVE, 1, 6, 6), (SEND, 1, 6, 7, 6), (READY, 5), (ARRIVE, 1, 11, 1), (ARRIVE, 0, 9, 4), (ARRIVE, 0, 7, 4),
    (SEND, 0, 8, 9, 3), (SEND, 0, 7, 10, 4), (SEND, 0, 4, 8, 6), (SEND, 0, 5, 11, 3), (SEND, 0, 9, 8, 4),
    (SEND, 0, 5, 9, 6), (ARRIVE, 1, 10, 2), (ARRIVE, 1, 8, 3), (ARRIVE, 1, 6, 5), (ARRIVE, 0, 11, 2),
    (ARRIVE, 1, 7, 4), (ARRIVE, 1, 9, 5), (SEND, 1, 8, 9, 3), (SEND, 1, 7, 10, 4), (SEND, 1, 4, 8, 6),
    (SEND, 1, 5, 11, 4), (SEND, 1, 9, 8, 5), (PAIRS, 5, (0, 1, 2)), (ARRIVE, 0, 10, 3), (ARRIVE, 1, 8, 4),
    (ARRIVE, 0, 6, 5), (ARRIVE, 1, 11, 2), (ARRIVE, 0, 9, 5), (ARRIVE, 0, 7, 6), (SEND, 1, 8, 9, 4),
    (SEND, 0, 7, 10, 6), (SEND, 0, 5, 11, 4), (READY, 6), (ARRIVE, 1, 9, 2), (ARRIVE, 1, 10, 3), (ARRIVE, 0, 8, 5),
    (ARRIVE, 1, 11, 3), (ARRIVE, 1, 9, 6), (ARRIVE, 1, 7, 6), (SEND, 1, 7, 10, 6), (SEND, 1, 5, 11, 5),
    (PAIRS, 6, (1, 4, 5)), (ARRIVE, 0, 9, 3), (ARRIVE, 0, 10, 4), (ARRIVE, 0, 8, 6), (READY, 7), (ARRIVE, 0, 11, 3),
    (ARRIVE, 0, 8, 4), (ARRIVE, 0, 9, 6), (SEND, 0, 5, 11, 5), (ARRIVE, 1, 9, 3), (ARRIVE, 1, 10, 4),
    (ARRIVE, 1, 8, 6), (ARRIVE, 1, 11, 4), (ARRIVE, 1, 8, 5), (SEND, 1, 5, 11, 6), (PAIRS, 7, (4, 5)),
    (ARRIVE, 1, 9, 4), (ARRIVE, 0, 10, 6), (READY, 8), (ARRIVE, 0, 11, 4), (SEND, 0, 5, 11, 6), (READY, 9),
    (ARRIVE, 1, 10, 6), (ARRIVE, 1, 11, 5), (PAIRS, 9, (0, 2, 6)), (READY, 10), (ARRIVE, 0, 11, 5),
    (ARRIVE, 1, 11, 6), (PAIRS, 10, (3, 4, 5)), (ARRIVE, 0, 11, 6), (PAIRS, 10, (8, 9)), (READY, 11),
    (PAIRS, 11, (1, 3, 6)), (PAIRS, 8, (2, 11)), (SHARED, 9, (7,), 0), (SHARED, 9, (3,), 2), (SHARED, 9, (1,), 0),
    (SHARED, 8, (6,), 1), (SHARED, 7, (3,), 0), (SHARED, 7, (1,), 1), (SHARED, 3, (1,), 0),
)

ROWS = 448
WINDOW = 128
CLUSTERS = 8
NONE = 1 << 20


def place():
    row, grp = lax.axis_index("row"), lax.axis_index("grp")
    return grp // 4, row // 2, grp % 4, row % 2


def device(x, y, z, core):
    return (lax.rem(y + 4, 4) * 2 + core, lax.rem(x + 4, 4) * 4 + lax.rem(z + 4, 4))


def scores(left, right):
    return lax.dot_general(
        left, right, (((1,), (1,)), ((), ())), preferred_element_type=jnp.float32
    )


def kernel(emb, scales, cid, rank, out, *refs):
    own, sib = refs[:SLOTS], refs[SLOTS : 2 * SLOTS]
    (
        unit, table, meta_own, meta_sib, first_own, first_sib, col, row_best, col_best, gathered, outgoing, incoming,
        recv, recv_meta, sib_recv, sib_recv_meta, sent, sent_meta, sib_sent, sib_sent_meta, local, back_sent, back_recv,
    ) = refs[2 * SLOTS :]
    x, y, z, core = place()
    chunk_rows = ROWS // CHUNKS
    def other():
        return device(x, y, z, 1 - core)

    barrier = pltpu.get_barrier_semaphore()
    for dx, dy, dz in ((1, 0, 0), (-1, 0, 0), (0, 1, 0), (0, -1, 0), (0, 0, 1), (0, 0, -1)):
        pl.semaphore_signal(
            barrier, inc=1, device_id=device(x + dx, y + dy, z + dz, core), device_id_type=MESH
        )
    pl.semaphore_signal(barrier, inc=1, device_id=other(), device_id_type=MESH)

    def clear(i, _):
        row_best[i] = jnp.full((2 * WINDOW, WINDOW), -1.0, jnp.float32)
        col_best[i] = jnp.full((8, 2 * WINDOW), -1.0, jnp.float32)
        return 0

    lax.fori_loop(0, SLOTS * 4, clear, 0)

    total = jnp.zeros((ROWS, 1), jnp.float32)
    for b in range(8):
        part = emb[:, b * 128 : (b + 1) * 128].astype(jnp.float32) * scales[:, b : b + 1]
        total = total + jnp.sum(part * part, axis=1, keepdims=True)
    inverse = lax.rsqrt(total + 1e-06)
    for b in range(8):
        part = emb[:, b * 128 : (b + 1) * 128].astype(jnp.float32) * scales[:, b : b + 1]
        unit[:, b * 128 : (b + 1) * 128] = (part * inverse).astype(jnp.bfloat16)

    cids, ranks = cid[...], rank[...]
    sub16 = lax.broadcasted_iota(jnp.int32, (16, ROWS), 0)
    member = sub16 == cids
    earlier = (
        lax.broadcasted_iota(jnp.int32, (ROWS, ROWS), 0) < lax.broadcasted_iota(jnp.int32, (ROWS, ROWS), 1)
    )
    before = jnp.dot(
        jnp.where(member, 1.0, 0.0).astype(jnp.bfloat16),
        jnp.where(earlier, 1.0, 0.0).astype(jnp.bfloat16),
        preferred_element_type=jnp.float32,
    )
    sub128 = lax.broadcasted_iota(jnp.int32, (WINDOW, ROWS), 0)
    start = jnp.sum(jnp.where(cids < sub128, 1, 0), axis=1, keepdims=True)
    position = jnp.sum(
        jnp.where(member, before + start[0:16].astype(jnp.float32), 0.0), axis=0, keepdims=True
    ).astype(jnp.int32)
    tile_start = jnp.minimum(start >> 4, (ROWS - WINDOW) // 16)
    window_start = tile_start * 16
    diagonal = lax.broadcasted_iota(jnp.int32, (WINDOW, WINDOW), 0) == lax.broadcasted_iota(
        jnp.int32, (WINDOW, WINDOW), 1
    )
    start_row = jnp.sum(jnp.where(diagonal, tile_start, 0), axis=0, keepdims=True)
    for c in range(CLUSTERS):
        spot = window_start[c : c + 1, :] + lax.broadcasted_iota(jnp.int32, (WINDOW, ROWS), 0)
        hit = jnp.logical_and(spot == position, cids == c)
        table[c * WINDOW : (c + 1) * WINDOW, :] = jnp.where(hit, 1.0, 0.0).astype(jnp.bfloat16)
    digits = jnp.where(
        sub16 == 0, ranks >> 7, jnp.where(sub16 == 1, ranks & 127, jnp.where(sub16 == 2, 1, 0))
    ).astype(jnp.float32).astype(jnp.bfloat16)
    placed = scores(digits, table[...])
    slot_rank = jnp.where(placed[2:3] > 0.5, placed[0:1] * 128.0 + placed[1:2], float(NONE)).astype(jnp.int32)
    meta_own[0] = jnp.concatenate(
        [slot_rank[:, c * WINDOW : (c + 1) * WINDOW] for c in range(CLUSTERS)]
        + [start_row, jnp.zeros((7, WINDOW), jnp.int32)],
        axis=0,
    )

    def sort_chunk(k):
        spot = lax.broadcasted_iota(jnp.int32, (chunk_rows, ROWS), 0) + k * chunk_rows
        move = jnp.where(spot == position, 1.0, 0.0).astype(jnp.bfloat16)
        own[0][k * chunk_rows : (k + 1) * chunk_rows, :] = jnp.dot(
            move, unit[...], preferred_element_type=jnp.float32
        ).astype(jnp.bfloat16)

    def piece(ref, chunk):
        return ref.at[pl.ds(chunk * chunk_rows, chunk_rows)]

    def to_sibling(slot, chunk):
        return pltpu.make_async_remote_copy(
            src_ref=own[slot] if chunk is None else piece(own[slot], chunk),
            dst_ref=sib[slot] if chunk is None else piece(sib[slot], chunk),
            send_sem=sib_sent.at[slot], recv_sem=sib_recv.at[slot],
            device_id=other(), device_id_type=MESH,
        )

    def meta_to_sibling(slot):
        return pltpu.make_async_remote_copy(
            src_ref=meta_own.at[slot], dst_ref=meta_sib.at[slot],
            send_sem=sib_sent_meta.at[slot], recv_sem=sib_recv_meta.at[slot],
            device_id=other(), device_id_type=MESH,
        )

    def target(e, d):
        ux, uy, uz = (q - p for p, q in zip(OFFSETS[e], OFFSETS[d]))
        return device(x - ux, y - uy, z - uz, core)

    def along(e, d, chunk):
        return pltpu.make_async_remote_copy(
            src_ref=own[e] if chunk is None else piece(own[e], chunk),
            dst_ref=own[d] if chunk is None else piece(own[d], chunk),
            send_sem=sent.at[d - 1],
            recv_sem=recv.at[(d - 1) * CHUNKS + (chunk or 0)],
            device_id=target(e, d), device_id_type=MESH,
        )

    def meta_along(e, d):
        return pltpu.make_async_remote_copy(
            src_ref=meta_own.at[e], dst_ref=meta_own.at[d],
            send_sem=sent_meta.at[d - 1], recv_sem=recv_meta.at[d - 1],
            device_id=target(e, d), device_id_type=MESH,
        )

    def starts_to_scalars(slot):
        return [
            pltpu.make_async_copy(meta.at[slot, pl.ds(8, 1)], first.at[slot], local.at[slot * 2 + n])
            for n, (meta, first) in enumerate(((meta_own, first_own), (meta_sib, first_sib)))
        ]

    def arrive(c, slot, chunk):
        if slot == 0:
            if chunk == 0:
                meta_to_sibling(0).start()
        else:
            e = parent_of[(c, slot, chunk)]
            along(e, slot, chunk).wait_recv()
            if chunk == 0:
                meta_along(e, slot).wait_recv()
                meta_to_sibling(slot).start()
        to_sibling(slot, chunk).start()

    def send(c, e, d, chunk):
        if chunk == 0:
            meta_along(e, d).start()
        along(e, d, chunk).start()

    parent_of = {}
    for item in PLAN:
        if item[0] == SEND:
            _, c, e, d, chunk = item
            parent_of[(c, d, chunk)] = e

    def begin(slot):
        meta_to_sibling(slot).wait_recv()
        for copy in starts_to_scalars(slot):
            copy.start()
        for n, meta in enumerate((meta_own, meta_sib)):
            tile = meta[slot, 0:8, :]
            mine = jnp.where(core == 0, tile, jnp.concatenate([tile[4:8], tile[0:4]], axis=0))
            turned = mine.astype(jnp.float32).T
            for q in range(4):
                col[slot * 4 + q, pl.ds(n * WINDOW, WINDOW), :] = jnp.broadcast_to(
                    turned[:, q : q + 1], (WINDOW, WINDOW)
                )

    def ready(slot):
        to_sibling(slot, None).wait_recv()
        for copy in starts_to_scalars(slot):
            copy.wait()

    def window(slot, cluster):
        return [
            ref[pl.ds(first[slot, 0, cluster] * 16, WINDOW), :]
            for ref, first in ((own[slot], first_own), (sib[slot], first_sib))
        ]

    def pairs(b, group, count, base, itself=False):
        def one(i, _):
            q = base + i
            cluster = core * 4 + q
            right = jnp.concatenate(window(b, cluster), axis=0)
            left = jnp.concatenate([w for a in group for w in window(a, cluster)], axis=0)
            found = scores(left, right)
            right_rank = jnp.concatenate(
                [meta[b, pl.ds(cluster, 1), :] for meta in (meta_own, meta_sib)], axis=1
            ).astype(jnp.float32)
            for n, a in enumerate(group):
                value = found[n * 2 * WINDOW : (n + 1) * 2 * WINDOW]
                less = right_rank < jnp.concatenate([col[a * 4 + q]] * 2, axis=1)
                to_left = jnp.where(less, value, -1.0)
                row_best[a * 4 + q] = jnp.maximum(
                    row_best[a * 4 + q], jnp.maximum(to_left[:, :WINDOW], to_left[:, WINDOW:])
                )
                if not itself:
                    to_right = jnp.where(less, -1.0, value).reshape(2 * WINDOW // 8, 8, 2 * WINDOW)
                    col_best[b * 4 + q] = jnp.maximum(col_best[b * 4 + q], jnp.max(to_right, axis=0))
            return 0

        lax.fori_loop(0, count, one, 0, unroll=2)

    def on_core(c, steps):
        @pl.when(core == c)
        def _():
            for step in steps:
                step()

    pending = [[], []]

    def flush():
        for c in (0, 1):
            if pending[c]:
                on_core(c, pending[c])
            pending[c] = []

    pl.semaphore_wait(barrier, 7)
    for item in PLAN:
        if item[0] == ARRIVE:
            pending[item[1]].append(functools.partial(arrive, *item[1:]))
            continue
        if item[0] == SEND:
            pending[item[1]].append(functools.partial(send, *item[1:]))
            continue
        flush()
        if item[0] == SORT:
            sort_chunk(item[1])
        elif item[0] == BEGIN:
            begin(item[1])
        elif item[0] == READY:
            ready(item[1])
        elif item[0] == PAIRS:
            pairs(item[1], item[2], 4, 0)
        elif item[0] == SHARED:
            pairs(item[1], item[2], 2, (x, y, z)[item[3]] // 2 * 2)
        else:
            pairs(0, (0,), 4, 0, itself=True)
    flush()

    lane = lax.broadcasted_iota(jnp.int32, (2 * WINDOW, WINDOW), 1)

    def fold(i, best):
        for q in range(4):
            best = jnp.where(lane == i * 8 + q, jnp.max(row_best[i * 4 + q], axis=1, keepdims=True), best)
            gathered[pl.ds(i * 8 + q, 1), :] = jnp.max(col_best[i * 4 + q], axis=0, keepdims=True)
        for q in range(4, 8):
            gathered[pl.ds(i * 8 + q, 1), :] = jnp.full((1, 2 * WINDOW), -1.0, jnp.float32)
        return best

    best = lax.fori_loop(0, SLOTS, fold, jnp.full((2 * WINDOW, WINDOW), -1.0, jnp.float32))
    turned = best.T
    for n in (0, 1):
        half = jnp.maximum(
            turned[: SLOTS * 8, n * WINDOW : (n + 1) * WINDOW], gathered[:, n * WINDOW : (n + 1) * WINDOW]
        )
        outgoing[n] = half

    def reply(d, n):
        ox, oy, oz = OFFSETS[d]
        return pltpu.make_async_remote_copy(
            src_ref=outgoing.at[n, pl.ds(d * 8, 8)], dst_ref=incoming.at[n, pl.ds(d * 8, 8)],
            send_sem=back_sent.at[d * 2 + n], recv_sem=back_recv.at[d * 2 + n],
            device_id=device(x + ox, y + oy, z + oz, core if n == 0 else 1 - core), device_id_type=MESH,
        )

    replies = [(d, n) for d in range(SLOTS) for n in (0, 1) if d or n]
    for d, n in replies:
        reply(d, n).start()
    for d in range(1, SLOTS):
        along(0, d, None).wait_send()
        meta_along(0, d).wait_send()
    for d in range(SLOTS):
        to_sibling(d, None).wait_send()
        meta_to_sibling(d).wait_send()
    for d, n in replies:
        reply(d, n).wait_recv()
    final = []
    for n in (0, 1):
        best = outgoing[n, 0:8] if n == 0 else incoming[n, 0:8]
        for d in range(1, SLOTS):
            best = jnp.maximum(best, incoming[n, d * 8 : (d + 1) * 8])
        final.append(best)
    lower = jnp.where(core == 0, final[0], final[1])
    upper = jnp.where(core == 0, final[1], final[0])
    line = jnp.concatenate([lower[q : q + 1] for q in range(4)] + [upper[q : q + 1] for q in range(4)], axis=1)
    high = line.astype(jnp.bfloat16)
    rest = line - high.astype(jnp.float32)
    middle = rest.astype(jnp.bfloat16)
    low = (rest - middle.astype(jnp.float32)).astype(jnp.bfloat16)
    sub = lax.broadcasted_iota(jnp.int32, (16, CLUSTERS * WINDOW), 0)
    parts = jnp.where(
        sub == 0, high.astype(jnp.float32),
        jnp.where(sub == 1, middle.astype(jnp.float32), jnp.where(sub == 2, low.astype(jnp.float32), 0.0)),
    ).astype(jnp.bfloat16)
    out[...] = jnp.sum(jnp.dot(parts, table[...], preferred_element_type=jnp.float32), axis=0, keepdims=True)
    for d, n in replies:
        reply(d, n).wait_send()


def local(embeddings, scales, cluster_id, doc_rank):
    vmem = pl.BlockSpec(memory_space=pltpu.VMEM)
    dma = pltpu.SemaphoreType.DMA
    best = pl.pallas_call(
        kernel,
        out_shape=jax.ShapeDtypeStruct((1, ROWS), jnp.float32),
        in_specs=[vmem] * 4,
        out_specs=vmem,
        scratch_shapes=[pltpu.VMEM((ROWS, 1024), jnp.bfloat16)] * (2 * SLOTS)
        + [
            pltpu.VMEM((ROWS, 1024), jnp.bfloat16),
            pltpu.VMEM((CLUSTERS * WINDOW, ROWS), jnp.bfloat16),
            pltpu.VMEM((SLOTS, 16, WINDOW), jnp.int32),
            pltpu.VMEM((SLOTS, 16, WINDOW), jnp.int32),
            pltpu.SMEM((SLOTS, 1, WINDOW), jnp.int32),
            pltpu.SMEM((SLOTS, 1, WINDOW), jnp.int32),
            pltpu.VMEM((SLOTS * 4, 2 * WINDOW, WINDOW), jnp.float32),
            pltpu.VMEM((SLOTS * 4, 2 * WINDOW, WINDOW), jnp.float32),
            pltpu.VMEM((SLOTS * 4, 8, 2 * WINDOW), jnp.float32),
            pltpu.VMEM((SLOTS * 8, 2 * WINDOW), jnp.float32),
            pltpu.VMEM((2, SLOTS * 8, WINDOW), jnp.float32),
            pltpu.VMEM((2, SLOTS * 8, WINDOW), jnp.float32),
            dma(((SLOTS - 1) * CHUNKS,)),
            dma((SLOTS - 1,)),
            dma((SLOTS,)),
            dma((SLOTS,)),
            dma((SLOTS - 1,)),
            dma((SLOTS - 1,)),
            dma((SLOTS,)),
            dma((SLOTS,)),
            dma((2 * SLOTS,)),
            dma((2 * SLOTS,)),
            dma((2 * SLOTS,)),
        ],
        compiler_params=pltpu.CompilerParams(
            collective_id=0, has_side_effects=True, vmem_limit_bytes=56 * 2**20
        ),
        cost_estimate=pl.CostEstimate(flops=30 * 10**9, bytes_accessed=2**20, transcendentals=0),
        name="nearest_in_cluster",
    )(embeddings, scales, cluster_id.reshape(1, ROWS), doc_rank.reshape(1, ROWS))
    return best.reshape(ROWS)


def solution(mesh):
    return jax.shard_map(
        local,
        mesh=mesh,
        in_specs=(P(("row", "grp"), None), P(("row", "grp"), None), P(("row", "grp")), P(("row", "grp"))),
        out_specs=P(("row", "grp")),
        check_vma=False,
    )
```

```python
import functools

import jax
import jax.numpy as jnp
from jax import lax
from jax.experimental import pallas as pl
from jax.experimental.pallas import tpu as pltpu
from jax.sharding import PartitionSpec as P

MESH = pl.DeviceIdType.MESH

OFFSETS = (
    (0, 0, 0), (0, 1, 0), (0, 0, 3), (1, 0, 0), (3, 1, 0), (0, 0, 1), (3, 2, 0), (0, 0, 2), (0, 3, 2), (0, 3, 3),
    (2, 0, 0), (2, 2, 0),
)
SLOTS = len(OFFSETS)
ROOTS = (0, 1)
EXTRA = 1
CHUNKS = 7
SORT, ARRIVE, SEND, BEGIN, READY, PAIRS, SHARED, OWN, TABLE, FOLD = range(10)
PLAN = (
    (SORT, 0), (TABLE,), (ARRIVE, 0, 0, 0), (ARRIVE, 1, 1, 0), (SEND, 0, 0, 3, 0), (SEND, 0, 0, 1, 0),
    (SEND, 0, 0, 5, 0), (SEND, 0, 0, 2, 0), (SEND, 1, 1, 0, 0), (SEND, 1, 1, 4, 0), (SORT, 1), (SORT, 2),
    (ARRIVE, 0, 0, 1), (ARRIVE, 1, 1, 1), (SEND, 0, 0, 3, 1), (SEND, 0, 0, 1, 1), (SEND, 0, 0, 5, 1),
    (SEND, 1, 1, 0, 1), (SEND, 1, 1, 4, 1), (SORT, 3), (ARRIVE, 0, 0, 2), (ARRIVE, 1, 1, 2), (SEND, 0, 0, 3, 2),
    (SEND, 0, 0, 1, 2), (SEND, 0, 0, 5, 2), (SEND, 0, 0, 2, 2), (SEND, 1, 1, 0, 2), (SEND, 1, 1, 4, 2), (SORT, 4),
    (ARRIVE, 0, 0, 3), (ARRIVE, 1, 1, 3), (SEND, 0, 0, 2, 3), (SORT, 5), (ARRIVE, 0, 0, 4), (ARRIVE, 1, 1, 4),
    (SORT, 6), (ARRIVE, 0, 0, 5), (ARRIVE, 1, 1, 5), (SEND, 0, 0, 3, 3), (SEND, 0, 0, 1, 3), (SEND, 0, 0, 5, 3),
    (SEND, 1, 1, 0, 3), (SEND, 1, 1, 4, 3), (SEND, 0, 0, 2, 4), (ARRIVE, 0, 0, 6), (ARRIVE, 1, 1, 6),
    (SEND, 0, 0, 1, 4), (SEND, 1, 1, 0, 4), (ARRIVE, 0, 3, 0), (ARRIVE, 0, 1, 0), (ARRIVE, 0, 5, 0),
    (ARRIVE, 0, 2, 0), (ARRIVE, 1, 0, 0), (ARRIVE, 1, 4, 0), (SEND, 0, 1, 4, 0), (SEND, 1, 0, 3, 0),
    (SEND, 1, 0, 5, 0), (SEND, 1, 0, 2, 0), (SEND, 0, 0, 1, 5), (SEND, 1, 1, 0, 5), (ARRIVE, 0, 3, 1),
    (ARRIVE, 0, 1, 1), (ARRIVE, 0, 5, 1), (ARRIVE, 1, 0, 1), (ARRIVE, 1, 4, 1), (ARRIVE, 0, 2, 2),
    (SEND, 0, 1, 4, 1), (SEND, 0, 5, 7, 1), (SEND, 1, 0, 3, 1), (SEND, 1, 0, 2, 1), (SEND, 0, 2, 9, 0),
    (SEND, 1, 4, 6, 0), (SEND, 1, 0, 5, 1), (ARRIVE, 0, 3, 2), (ARRIVE, 0, 1, 2), (ARRIVE, 0, 5, 2),
    (ARRIVE, 1, 0, 2), (ARRIVE, 1, 4, 2), (ARRIVE, 0, 2, 3), (SEND, 0, 1, 4, 2), (SEND, 1, 0, 3, 2),
    (SEND, 1, 0, 2, 2), (BEGIN, 0), (BEGIN, 1), (SEND, 1, 0, 5, 2), (SEND, 0, 0, 1, 6), (SEND, 1, 1, 0, 6),
    (ARRIVE, 0, 3, 3), (ARRIVE, 0, 1, 3), (ARRIVE, 0, 5, 3), (ARRIVE, 1, 0, 3), (ARRIVE, 1, 4, 3), (ARRIVE, 0, 2, 4),
    (SEND, 0, 1, 4, 3), (SEND, 1, 0, 3, 3), (SEND, 1, 0, 2, 3), (SEND, 0, 5, 7, 3), (ARRIVE, 0, 4, 0),
    (ARRIVE, 1, 3, 0), (ARRIVE, 1, 5, 0), (ARRIVE, 1, 2, 0), (ARRIVE, 0, 1, 4), (ARRIVE, 1, 0, 4),
    (SEND, 0, 4, 6, 0), (SEND, 1, 2, 9, 0), (SEND, 0, 1, 4, 4), (SEND, 1, 0, 3, 4), (SEND, 1, 0, 2, 4),
    (SEND, 1, 4, 6, 1), (SEND, 0, 0, 3, 4), (SEND, 1, 1, 4, 4), (ARRIVE, 0, 4, 1), (ARRIVE, 0, 7, 1),
    (ARRIVE, 1, 3, 1), (ARRIVE, 1, 2, 1), (ARRIVE, 0, 1, 5), (ARRIVE, 1, 0, 5), (SEND, 0, 7, 2, 1),
    (SEND, 1, 2, 9, 1), (SEND, 1, 0, 2, 5), (SEND, 0, 4, 6, 1), (SEND, 0, 7, 8, 1), (SEND, 1, 0, 5, 3),
    (SEND, 0, 0, 2, 5), (SEND, 0, 1, 4, 5), (SEND, 1, 0, 3, 5), (ARRIVE, 0, 9, 0), (ARRIVE, 1, 6, 0),
    (ARRIVE, 1, 5, 1), (ARRIVE, 0, 4, 2), (ARRIVE, 1, 3, 2), (ARRIVE, 1, 2, 2), (BEGIN, 3), (BEGIN, 4),
    (SEND, 0, 4, 6, 2), (SEND, 0, 0, 3, 5), (SEND, 1, 1, 4, 5), (ARRIVE, 1, 5, 2), (ARRIVE, 0, 4, 3),
    (ARRIVE, 1, 3, 3), (ARRIVE, 1, 2, 3), (ARRIVE, 0, 1, 6), (ARRIVE, 1, 0, 6), (SEND, 1, 5, 7, 2),
    (SEND, 1, 2, 9, 3), (SEND, 1, 0, 2, 6), (BEGIN, 5), (SEND, 1, 4, 6, 2), (SEND, 0, 2, 9, 3), (SEND, 1, 0, 5, 4),
    (SEND, 0, 0, 3, 6), (SEND, 0, 0, 2, 6), (SEND, 1, 1, 4, 6), (READY, 0), (READY, 1), (ARRIVE, 0, 6, 0),
    (ARRIVE, 1, 9, 0), (ARRIVE, 0, 7, 3), (ARRIVE, 0, 4, 4), (ARRIVE, 1, 3, 4), (ARRIVE, 1, 2, 4),
    (SEND, 1, 2, 7, 0), (SEND, 1, 4, 6, 3), (SEND, 0, 0, 5, 4), (SEND, 0, 1, 4, 6), (SEND, 1, 0, 3, 6), (OWN, 0),
    (PAIRS, 1, (0,)), (ARRIVE, 0, 2, 1), (ARRIVE, 1, 9, 1), (ARRIVE, 1, 6, 1), (ARRIVE, 0, 3, 4), (ARRIVE, 1, 4, 4),
    (ARRIVE, 1, 2, 5), (SEND, 0, 2, 9, 1), (SEND, 0, 3, 10, 0), (SEND, 1, 6, 11, 0), (SEND, 1, 2, 7, 1),
    (SEND, 0, 4, 6, 3), (SEND, 1, 2, 9, 4), (SEND, 0, 0, 5, 5), (ARRIVE, 0, 6, 1), (ARRIVE, 0, 8, 1),
    (ARRIVE, 1, 5, 3), (ARRIVE, 0, 2, 5), (ARRIVE, 0, 4, 5), (ARRIVE, 1, 3, 5), (BEGIN, 2), (SEND, 0, 6, 11, 0),
    (SEND, 1, 3, 10, 0), (SEND, 0, 2, 7, 2), (SEND, 1, 4, 6, 4), (SEND, 1, 0, 5, 5), (ARRIVE, 0, 6, 2),
    (ARRIVE, 1, 7, 2), (ARRIVE, 1, 9, 3), (ARRIVE, 0, 3, 5), (ARRIVE, 1, 4, 5), (ARRIVE, 1, 2, 6),
    (SEND, 1, 7, 8, 2), (BEGIN, 6), (SEND, 0, 3, 10, 1), (SEND, 1, 6, 11, 1), (SEND, 1, 2, 7, 3), (SEND, 0, 4, 6, 4),
    (SEND, 1, 2, 9, 5), (SEND, 0, 0, 5, 6), (ARRIVE, 1, 6, 2), (ARRIVE, 0, 9, 3), (ARRIVE, 1, 5, 4),
    (ARRIVE, 0, 3, 6), (ARRIVE, 0, 2, 6), (ARRIVE, 1, 4, 6), (SEND, 1, 9, 8, 0), (SEND, 0, 6, 11, 1),
    (SEND, 1, 3, 10, 1), (SEND, 1, 4, 6, 5), (SEND, 0, 2, 9, 6), (SEND, 1, 0, 5, 6), (READY, 2), (PAIRS, 2, (0, 1)),
    (ARRIVE, 1, 7, 0), (ARRIVE, 0, 9, 1), (ARRIVE, 1, 6, 3), (ARRIVE, 0, 5, 4), (ARRIVE, 0, 4, 6), (ARRIVE, 1, 3, 6),
    (SEND, 0, 9, 8, 0), (SEND, 0, 6, 11, 2), (SEND, 1, 3, 10, 2), (SEND, 0, 4, 6, 5), (READY, 3), (READY, 4),
    (ARRIVE, 0, 10, 0), (ARRIVE, 1, 11, 0), (ARRIVE, 1, 7, 1), (ARRIVE, 0, 6, 3), (ARRIVE, 1, 9, 4),
    (ARRIVE, 0, 5, 5), (SEND, 1, 7, 8, 1), (SEND, 0, 5, 7, 5), (BEGIN, 9), (SEND, 0, 3, 10, 2), (SEND, 1, 6, 11, 2),
    (SEND, 0, 2, 7, 4), (SEND, 0, 4, 6, 6), (PAIRS, 4, (0, 1, 2)), (ARRIVE, 0, 11, 0), (ARRIVE, 1, 10, 0),
    (ARRIVE, 0, 7, 2), (ARRIVE, 1, 8, 2), (ARRIVE, 1, 6, 4), (ARRIVE, 1, 5, 5), (SEND, 0, 7, 8, 2),
    (SEND, 1, 8, 9, 2), (BEGIN, 7), (SEND, 0, 3, 10, 3), (SEND, 1, 6, 11, 3), (SEND, 1, 2, 7, 4), (SEND, 1, 2, 9, 6),
    (SEND, 1, 4, 6, 6), (ARRIVE, 0, 10, 1), (ARRIVE, 1, 11, 1), (ARRIVE, 1, 7, 3), (ARRIVE, 0, 6, 4),
    (ARRIVE, 1, 9, 5), (ARRIVE, 0, 5, 6), (SEND, 0, 5, 7, 6), (SEND, 0, 6, 11, 3), (SEND, 1, 3, 10, 3),
    (SEND, 1, 2, 7, 5), (PAIRS, 3, (2, 4)), (ARRIVE, 1, 8, 0), (ARRIVE, 0, 11, 1), (ARRIVE, 1, 10, 1),
    (ARRIVE, 1, 6, 5), (ARRIVE, 0, 9, 6), (ARRIVE, 1, 5, 6), (SEND, 1, 5, 7, 6), (SEND, 0, 9, 8, 3),
    (SEND, 0, 3, 10, 4), (SEND, 1, 6, 11, 4), (READY, 5), (ARRIVE, 0, 8, 0), (ARRIVE, 1, 8, 1), (ARRIVE, 0, 11, 2),
    (ARRIVE, 1, 10, 2), (ARRIVE, 0, 7, 5), (ARRIVE, 0, 6, 5), (SEND, 0, 8, 7, 0), (SEND, 0, 7, 8, 5), (BEGIN, 10),
    (BEGIN, 11), (SEND, 1, 9, 8, 3), (SEND, 0, 6, 11, 4), (SEND, 1, 3, 10, 4), (PAIRS, 5, (1, 3, 4)),
    (ARRIVE, 0, 10, 2), (ARRIVE, 0, 8, 2), (ARRIVE, 1, 9, 2), (ARRIVE, 1, 11, 2), (ARRIVE, 0, 7, 4),
    (ARRIVE, 0, 6, 6), (SEND, 0, 8, 9, 2), (SEND, 0, 7, 8, 4), (BEGIN, 8), (SEND, 1, 9, 8, 4), (SEND, 0, 3, 10, 5),
    (SEND, 1, 6, 11, 5), (ARRIVE, 0, 10, 3), (ARRIVE, 1, 11, 3), (ARRIVE, 1, 7, 4), (ARRIVE, 0, 7, 6),
    (ARRIVE, 1, 9, 6), (ARRIVE, 1, 6, 6), (SEND, 0, 7, 8, 6), (SEND, 0, 6, 11, 5), (SEND, 1, 3, 10, 5),
    (SEND, 1, 9, 8, 6), (READY, 6), (ARRIVE, 0, 11, 3), (ARRIVE, 1, 10, 3), (ARRIVE, 1, 7, 5), (ARRIVE, 1, 7, 6),
    (SEND, 1, 7, 8, 5), (SEND, 0, 3, 10, 6), (SEND, 1, 6, 11, 6), (PAIRS, 6, (0, 2, 5)), (FOLD, (5,)),
    (ARRIVE, 0, 7, 0), (ARRIVE, 0, 8, 5), (SEND, 0, 8, 9, 5), (ARRIVE, 0, 8, 3), (ARRIVE, 0, 10, 4),
    (ARRIVE, 1, 11, 4), (SEND, 0, 6, 11, 6), (SEND, 1, 3, 10, 6), (READY, 7), (ARRIVE, 0, 9, 2), (ARRIVE, 0, 8, 4),
    (SEND, 0, 8, 9, 4), (ARRIVE, 1, 8, 3), (ARRIVE, 0, 11, 4), (ARRIVE, 1, 10, 4), (PAIRS, 7, (1, 3, 4)),
    (ARRIVE, 0, 8, 6), (ARRIVE, 1, 8, 4), (ARRIVE, 0, 10, 5), (ARRIVE, 1, 11, 5), (PAIRS, 7, (6,)),
    (ARRIVE, 1, 8, 5), (ARRIVE, 0, 11, 5), (ARRIVE, 1, 10, 5), (ARRIVE, 1, 8, 6), (SHARED, 7, (0,), 2),
    (ARRIVE, 0, 9, 5), (SHARED, 6, (3,), 0), (READY, 8), (ARRIVE, 0, 10, 6), (ARRIVE, 1, 11, 6), (PAIRS, 8, (3,)),
    (ARRIVE, 0, 9, 4), (SHARED, 8, (1,), 1), (ARRIVE, 0, 11, 6), (ARRIVE, 1, 10, 6), (READY, 9),
    (PAIRS, 9, (1, 3, 6)), (FOLD, (1, 3, 6)), (READY, 10), (READY, 11), (PAIRS, 11, (2, 8, 9)), (FOLD, (8,)),
    (PAIRS, 10, (2, 4, 9)), (FOLD, (2, 4, 9)), (SHARED, 11, (10,), 1), (SHARED, 11, (7,), 0), (FOLD, (11,)),
    (SHARED, 10, (7,), 0), (FOLD, (7,)), (SHARED, 10, (0,), 0), (FOLD, (0, 10)),
)

ROWS = 448
WINDOW = 128
CLUSTERS = 8
NONE = 1 << 20


def place():
    row, grp = lax.axis_index("row"), lax.axis_index("grp")
    return grp // 4, row // 2, grp % 4, row % 2


def device(x, y, z, core):
    return (lax.rem(y + 4, 4) * 2 + core, lax.rem(x + 4, 4) * 4 + lax.rem(z + 4, 4))


def scores(left, right):
    return lax.dot_general(
        left, right, (((1,), (1,)), ((), ())), preferred_element_type=jnp.float32
    )


def kernel(emb, scales, cid, rank, out, *refs):
    own, sib = refs[:SLOTS], refs[SLOTS : 2 * SLOTS]
    (
        unit, table, meta_own, meta_sib, first_own, first_sib, col, row_best, col_best, outgoing, incoming,
        recv, recv_meta, sib_recv, sib_recv_meta, sent, sent_meta, sib_sent, sib_sent_meta, local, back_sent, back_recv,
    ) = refs[2 * SLOTS :]
    x, y, z, core = place()
    root = ROOTS[0] + core * (ROOTS[1] - ROOTS[0])
    chunk_rows = ROWS // CHUNKS
    def other():
        return device(x, y, z, 1 - core)

    barrier = pltpu.get_barrier_semaphore()
    for dx, dy, dz in ((1, 0, 0), (-1, 0, 0), (0, 1, 0), (0, -1, 0), (0, 0, 1), (0, 0, -1)):
        pl.semaphore_signal(
            barrier, inc=1, device_id=device(x + dx, y + dy, z + dz, core), device_id_type=MESH
        )
    pl.semaphore_signal(barrier, inc=1, device_id=other(), device_id_type=MESH)

    def clear(i, _):
        row_best[i] = jnp.full((2 * WINDOW, WINDOW), -1.0, jnp.float32)
        col_best[i] = jnp.full((8, 2 * WINDOW), -1.0, jnp.float32)
        return 0

    lax.fori_loop(0, SLOTS * 4, clear, 0)

    factor = scales[...].T
    total = jnp.zeros((ROWS, 1), jnp.float32)
    for b in range(8):
        part = emb[:, b * 128 : (b + 1) * 128].astype(jnp.float32) * factor[:, b : b + 1]
        total = total + jnp.sum(part * part, axis=1, keepdims=True)
    inverse = lax.rsqrt(total + 1e-06)
    for b in range(8):
        part = emb[:, b * 128 : (b + 1) * 128].astype(jnp.float32) * factor[:, b : b + 1]
        unit[:, b * 128 : (b + 1) * 128] = (part * inverse).astype(jnp.bfloat16)

    cids, ranks = cid[...], rank[...]
    sub16 = lax.broadcasted_iota(jnp.int32, (16, ROWS), 0)
    member = sub16 == cids
    earlier = (
        lax.broadcasted_iota(jnp.int32, (ROWS, ROWS), 0) < lax.broadcasted_iota(jnp.int32, (ROWS, ROWS), 1)
    )
    before = jnp.dot(
        jnp.where(member, 1.0, 0.0).astype(jnp.bfloat16),
        jnp.where(earlier, 1.0, 0.0).astype(jnp.bfloat16),
        preferred_element_type=jnp.float32,
    )
    sub128 = lax.broadcasted_iota(jnp.int32, (WINDOW, ROWS), 0)
    start = jnp.sum(jnp.where(cids < sub128, 1, 0), axis=1, keepdims=True)
    position = jnp.sum(
        jnp.where(member, before + start[0:16].astype(jnp.float32), 0.0), axis=0, keepdims=True
    ).astype(jnp.int32)
    tile_start = jnp.minimum(start >> 4, (ROWS - WINDOW) // 16)
    window_start = tile_start * 16
    diagonal = lax.broadcasted_iota(jnp.int32, (WINDOW, WINDOW), 0) == lax.broadcasted_iota(
        jnp.int32, (WINDOW, WINDOW), 1
    )
    start_row = jnp.sum(jnp.where(diagonal, tile_start, 0), axis=0, keepdims=True)
    def make_table():
        for c in range(CLUSTERS):
            spot = window_start[c : c + 1, :] + lax.broadcasted_iota(jnp.int32, (WINDOW, ROWS), 0)
            hit = jnp.logical_and(spot == position, cids == c)
            table[c * WINDOW : (c + 1) * WINDOW, :] = jnp.where(hit, 1.0, 0.0).astype(jnp.bfloat16)
        digits = jnp.where(
            sub16 == 0, ranks >> 7, jnp.where(sub16 == 1, ranks & 127, jnp.where(sub16 == 2, 1, 0))
        ).astype(jnp.float32).astype(jnp.bfloat16)
        placed = scores(digits, table[...])
        slot_rank = jnp.where(placed[2:3] > 0.5, placed[0:1] * 128.0 + placed[1:2], float(NONE)).astype(jnp.int32)
        meta_own[root] = jnp.concatenate(
            [slot_rank[:, c * WINDOW : (c + 1) * WINDOW] for c in range(CLUSTERS)]
            + [start_row, jnp.zeros((7, WINDOW), jnp.int32)],
            axis=0,
        )

    def sort_chunk(k):
        spot = lax.broadcasted_iota(jnp.int32, (chunk_rows, ROWS), 0) + k * chunk_rows
        move = jnp.where(spot == position, 1.0, 0.0).astype(jnp.bfloat16)
        rows = jnp.dot(move, unit[...], preferred_element_type=jnp.float32).astype(jnp.bfloat16)
        for c in (0, 1):

            @pl.when(core == c)
            def _():
                own[ROOTS[c]][k * chunk_rows : (k + 1) * chunk_rows, :] = rows

    def piece(ref, chunk):
        return ref.at[pl.ds(chunk * chunk_rows, chunk_rows)]

    def to_sibling(slot, chunk):
        return pltpu.make_async_remote_copy(
            src_ref=own[slot] if chunk is None else piece(own[slot], chunk),
            dst_ref=sib[slot] if chunk is None else piece(sib[slot], chunk),
            send_sem=sib_sent.at[slot], recv_sem=sib_recv.at[slot],
            device_id=other(), device_id_type=MESH,
        )

    def meta_to_sibling(slot):
        return pltpu.make_async_remote_copy(
            src_ref=meta_own.at[slot], dst_ref=meta_sib.at[slot],
            send_sem=sib_sent_meta.at[slot], recv_sem=sib_recv_meta.at[slot],
            device_id=other(), device_id_type=MESH,
        )

    def target(e, d):
        ux, uy, uz = (q - p for p, q in zip(OFFSETS[e], OFFSETS[d]))
        return device(x - ux, y - uy, z - uz, core)

    def along(e, d, chunk):
        return pltpu.make_async_remote_copy(
            src_ref=own[e] if chunk is None else piece(own[e], chunk),
            dst_ref=own[d] if chunk is None else piece(own[d], chunk),
            send_sem=sent.at[d],
            recv_sem=recv.at[d * CHUNKS + (chunk or 0)],
            device_id=target(e, d), device_id_type=MESH,
        )

    def meta_along(e, d):
        return pltpu.make_async_remote_copy(
            src_ref=meta_own.at[e], dst_ref=meta_own.at[d],
            send_sem=sent_meta.at[d], recv_sem=recv_meta.at[d],
            device_id=target(e, d), device_id_type=MESH,
        )

    def starts_to_scalars(slot):
        return [
            pltpu.make_async_copy(meta.at[slot, pl.ds(8, 1)], first.at[slot], local.at[slot * 2 + n])
            for n, (meta, first) in enumerate(((meta_own, first_own), (meta_sib, first_sib)))
        ]

    def arrive(c, slot, chunk):
        if slot != ROOTS[c]:
            e = parent_of[(c, slot, chunk)]
            along(e, slot, chunk).wait_recv()
            if chunk == EXTRA:
                meta_along(e, slot).wait_recv()
        if chunk == EXTRA:
            meta_to_sibling(slot).start()
        to_sibling(slot, chunk).start()

    def send(c, e, d, chunk):
        if chunk == EXTRA:
            meta_along(e, d).start()
        along(e, d, chunk).start()

    parent_of = {}
    for item in PLAN:
        if item[0] == SEND:
            _, c, e, d, chunk = item
            parent_of[(c, d, chunk)] = e

    def begin(slot):
        meta_to_sibling(slot).wait_recv()
        for copy in starts_to_scalars(slot):
            copy.start()
        for n, meta in enumerate((meta_own, meta_sib)):
            tile = meta[slot, 0:8, :]
            mine = jnp.where(core == 0, tile, jnp.concatenate([tile[4:8], tile[0:4]], axis=0))
            turned = mine.astype(jnp.float32).T
            for q in range(4):
                col[slot * 4 + q, pl.ds(n * WINDOW, WINDOW), :] = jnp.broadcast_to(
                    turned[:, q : q + 1], (WINDOW, WINDOW)
                )

    def ready(slot):
        to_sibling(slot, None).wait_recv()
        for copy in starts_to_scalars(slot):
            copy.wait()

    def window(slot, cluster):
        return [
            ref[pl.ds(first[slot, 0, cluster] * 16, WINDOW), :]
            for ref, first in ((own[slot], first_own), (sib[slot], first_sib))
        ]

    def pairs(b, group, count, base, itself=False):
        def one(i, _):
            q = base + i
            cluster = core * 4 + q
            right = jnp.concatenate(window(b, cluster), axis=0)
            left = jnp.concatenate([w for a in group for w in window(a, cluster)], axis=0)
            found = scores(left, right)
            right_rank = jnp.concatenate(
                [meta[b, pl.ds(cluster, 1), :] for meta in (meta_own, meta_sib)], axis=1
            ).astype(jnp.float32)
            for n, a in enumerate(group):
                value = found[n * 2 * WINDOW : (n + 1) * 2 * WINDOW]
                less = right_rank < jnp.concatenate([col[a * 4 + q]] * 2, axis=1)
                to_left = jnp.where(less, value, -1.0)
                row_best[a * 4 + q] = jnp.maximum(
                    row_best[a * 4 + q], jnp.maximum(to_left[:, :WINDOW], to_left[:, WINDOW:])
                )
                if not itself:
                    to_right = jnp.where(less, -1.0, value).reshape(2 * WINDOW // 8, 8, 2 * WINDOW)
                    col_best[b * 4 + q] = jnp.maximum(col_best[b * 4 + q], jnp.max(to_right, axis=0))
            return 0

        lax.fori_loop(0, count, one, 0, unroll=4)

    def on_core(c, steps):
        @pl.when(core == c)
        def _():
            for step in steps:
                step()

    def sent_to(d):
        along((d + 1) % SLOTS, d, None).wait_send()
        meta_along((d + 1) % SLOTS, d).wait_send()

    def reply(d, n):
        away = [[q - p for p, q in zip(OFFSETS[ROOTS[c]], OFFSETS[d])] for c in (n, 1 - n)]
        ox, oy, oz = (first + core * (second - first) for first, second in zip(*away))
        return pltpu.make_async_remote_copy(
            src_ref=outgoing.at[n * SLOTS + d], dst_ref=incoming.at[n * SLOTS + d],
            send_sem=back_sent.at[d * 2 + n], recv_sem=back_recv.at[d * 2 + n],
            device_id=device(x + ox, y + oy, z + oz, core if n == 0 else 1 - core), device_id_type=MESH,
        )

    def replies(d, what):
        if d not in ROOTS:
            getattr(reply(d, 0), what)()
        elif ROOTS[0] != ROOTS[1]:
            on_core(1 - ROOTS.index(d), [getattr(reply(d, 0), what)])
        getattr(reply(d, 1), what)()

    lane = lax.broadcasted_iota(jnp.int32, (2 * WINDOW, WINDOW), 1)

    def fold(group):
        best = jnp.full((2 * WINDOW, WINDOW), -1.0, jnp.float32)
        for n, d in enumerate(group):
            for q in range(4):
                best = jnp.where(lane == n * 8 + q, jnp.max(row_best[d * 4 + q], axis=1, keepdims=True), best)
        turned = best.T
        for n, d in enumerate(group):
            rows = jnp.concatenate(
                [jnp.max(col_best[d * 4 + q], axis=0, keepdims=True) for q in range(4)]
                + [jnp.full((4, 2 * WINDOW), -1.0, jnp.float32)],
                axis=0,
            )
            rows = jnp.maximum(rows, turned[n * 8 : (n + 1) * 8])
            for half in (0, 1):
                outgoing[half * SLOTS + d] = rows[:, half * WINDOW : (half + 1) * WINDOW]
            replies(d, "start")

    pending = [[], []]

    def flush():
        for c in (0, 1):
            if pending[c]:
                on_core(c, pending[c])
            pending[c] = []

    pl.semaphore_wait(barrier, 7)
    for item in PLAN:
        if item[0] == ARRIVE:
            pending[item[1]].append(functools.partial(arrive, *item[1:]))
            continue
        if item[0] == SEND:
            pending[item[1]].append(functools.partial(send, *item[1:]))
            continue
        flush()
        if item[0] == SORT:
            sort_chunk(item[1])
        elif item[0] == TABLE:
            make_table()
        elif item[0] == BEGIN:
            begin(item[1])
        elif item[0] == READY:
            ready(item[1])
        elif item[0] == PAIRS:
            pairs(item[1], item[2], 4, 0)
        elif item[0] == SHARED:
            pairs(item[1], item[2], 2, (x, y, z)[item[3]] // 2 * 2)
        elif item[0] == FOLD:
            fold(item[1])
        else:
            pairs(item[1], (item[1],), 4, 0, itself=True)
    flush()

    for d in range(SLOTS):
        to_sibling(d, None).wait_send()
        meta_to_sibling(d).wait_send()
        if d not in ROOTS:
            sent_to(d)
        elif ROOTS[0] != ROOTS[1]:
            on_core(1 - ROOTS.index(d), [functools.partial(sent_to, d)])
    for d in range(SLOTS):
        replies(d, "wait_recv")
    incoming[root] = outgoing[root]
    final = []
    for n in (0, 1):
        best = incoming[n * SLOTS]
        for d in range(1, SLOTS):
            best = jnp.maximum(best, incoming[n * SLOTS + d])
        final.append(best)
    lower = jnp.where(core == 0, final[0], final[1])
    upper = jnp.where(core == 0, final[1], final[0])
    line = jnp.concatenate([lower[q : q + 1] for q in range(4)] + [upper[q : q + 1] for q in range(4)], axis=1)
    high = line.astype(jnp.bfloat16)
    rest = line - high.astype(jnp.float32)
    middle = rest.astype(jnp.bfloat16)
    low = (rest - middle.astype(jnp.float32)).astype(jnp.bfloat16)
    sub = lax.broadcasted_iota(jnp.int32, (16, CLUSTERS * WINDOW), 0)
    parts = jnp.where(
        sub == 0, high.astype(jnp.float32),
        jnp.where(sub == 1, middle.astype(jnp.float32), jnp.where(sub == 2, low.astype(jnp.float32), 0.0)),
    ).astype(jnp.bfloat16)
    out[...] = jnp.sum(jnp.dot(parts, table[...], preferred_element_type=jnp.float32), axis=0, keepdims=True)
    for d in range(SLOTS):
        replies(d, "wait_send")


def local(embeddings, scales, cluster_id, doc_rank):
    vmem = pl.BlockSpec(memory_space=pltpu.VMEM)
    dma = pltpu.SemaphoreType.DMA
    best = pl.pallas_call(
        kernel,
        out_shape=jax.ShapeDtypeStruct((1, ROWS), jnp.float32),
        in_specs=[vmem] * 4,
        out_specs=vmem,
        scratch_shapes=[pltpu.VMEM((ROWS, 1024), jnp.bfloat16)] * (2 * SLOTS)
        + [
            pltpu.VMEM((ROWS, 1024), jnp.bfloat16),
            pltpu.VMEM((CLUSTERS * WINDOW, ROWS), jnp.bfloat16),
            pltpu.VMEM((SLOTS, 16, WINDOW), jnp.int32),
            pltpu.VMEM((SLOTS, 16, WINDOW), jnp.int32),
            pltpu.SMEM((SLOTS, 1, WINDOW), jnp.int32),
            pltpu.SMEM((SLOTS, 1, WINDOW), jnp.int32),
            pltpu.VMEM((SLOTS * 4, 2 * WINDOW, WINDOW), jnp.float32),
            pltpu.VMEM((SLOTS * 4, 2 * WINDOW, WINDOW), jnp.float32),
            pltpu.VMEM((SLOTS * 4, 8, 2 * WINDOW), jnp.float32),
            pltpu.VMEM((2 * SLOTS, 8, WINDOW), jnp.float32),
            pltpu.VMEM((2 * SLOTS, 8, WINDOW), jnp.float32),
            dma((SLOTS * CHUNKS,)),
            dma((SLOTS,)),
            dma((SLOTS,)),
            dma((SLOTS,)),
            dma((SLOTS,)),
            dma((SLOTS,)),
            dma((SLOTS,)),
            dma((SLOTS,)),
            dma((2 * SLOTS,)),
            dma((2 * SLOTS,)),
            dma((2 * SLOTS,)),
        ],
        compiler_params=pltpu.CompilerParams(
            collective_id=0, has_side_effects=True, vmem_limit_bytes=56 * 2**20
        ),
        cost_estimate=pl.CostEstimate(flops=30 * 10**9, bytes_accessed=2**20, transcendentals=0),
        name="nearest_in_cluster",
    )(embeddings, scales.T, cluster_id.reshape(1, ROWS), doc_rank.reshape(1, ROWS))
    return best.reshape(ROWS)


def solution(mesh):
    return jax.shard_map(
        local,
        mesh=mesh,
        in_specs=(P(("row", "grp"), None), P(("row", "grp"), None), P(("row", "grp")), P(("row", "grp"))),
        out_specs=P(("row", "grp")),
        check_vma=False,
    )
```

```python
import functools

import jax
import jax.numpy as jnp
from jax import lax
from jax.experimental import pallas as pl
from jax.experimental.pallas import tpu as pltpu
from jax.sharding import PartitionSpec as P

MESH = pl.DeviceIdType.MESH

OFFSETS = (
    (0, 0, 0), (0, 1, 0), (0, 0, 3), (1, 0, 0), (3, 1, 0), (0, 0, 1), (3, 2, 0), (0, 0, 2), (0, 3, 2), (0, 3, 3),
    (2, 0, 0), (2, 2, 0),
)
SLOTS = len(OFFSETS)
ROOTS = (0, 1)
EXTRA = 2
CHUNKS = 7
SORT, ARRIVE, SEND, BEGIN, READY, PAIRS, SHARED, OWN, TABLE, FOLD = range(10)
PLAN = (
    (SORT, 0), (SORT, 1), (ARRIVE, 0, 0, 0), (ARRIVE, 1, 1, 0), (SEND, 0, 0, 3, 0), (SEND, 0, 0, 1, 0),
    (SEND, 0, 0, 5, 0), (SEND, 0, 0, 2, 0), (SEND, 1, 1, 0, 0), (SEND, 1, 1, 4, 0), (TABLE,), (ARRIVE, 0, 0, 1),
    (ARRIVE, 1, 1, 1), (SEND, 0, 0, 3, 1), (SEND, 0, 0, 1, 1), (SEND, 0, 0, 5, 1), (SEND, 1, 1, 0, 1),
    (SEND, 1, 1, 4, 1), (SORT, 2), (SORT, 3), (ARRIVE, 0, 0, 2), (ARRIVE, 1, 1, 2), (SEND, 0, 0, 3, 2),
    (SEND, 0, 0, 1, 2), (SEND, 0, 0, 5, 2), (SEND, 0, 0, 2, 2), (SEND, 1, 1, 0, 2), (SEND, 1, 1, 4, 2), (SORT, 4),
    (ARRIVE, 0, 0, 3), (ARRIVE, 1, 1, 3), (SEND, 0, 0, 2, 3), (SORT, 5), (ARRIVE, 0, 0, 4), (ARRIVE, 1, 1, 4),
    (SORT, 6), (ARRIVE, 0, 0, 5), (ARRIVE, 1, 1, 5), (SEND, 0, 0, 3, 3), (SEND, 0, 0, 1, 3), (SEND, 0, 0, 5, 3),
    (SEND, 1, 1, 0, 3), (SEND, 1, 1, 4, 3), (SEND, 0, 0, 2, 4), (ARRIVE, 0, 0, 6), (ARRIVE, 1, 1, 6),
    (SEND, 0, 0, 1, 4), (SEND, 1, 1, 0, 4), (ARRIVE, 0, 3, 0), (ARRIVE, 0, 1, 0), (ARRIVE, 0, 5, 0),
    (ARRIVE, 0, 2, 0), (ARRIVE, 1, 0, 0), (ARRIVE, 1, 4, 0), (SEND, 0, 1, 4, 0), (SEND, 1, 0, 3, 0),
    (SEND, 1, 0, 5, 0), (SEND, 1, 0, 2, 0), (SEND, 0, 0, 1, 5), (SEND, 1, 1, 0, 5), (ARRIVE, 0, 3, 1),
    (ARRIVE, 0, 1, 1), (ARRIVE, 0, 5, 1), (ARRIVE, 1, 0, 1), (ARRIVE, 1, 4, 1), (ARRIVE, 0, 2, 2),
    (SEND, 0, 1, 4, 1), (SEND, 0, 5, 7, 1), (SEND, 1, 0, 3, 1), (SEND, 1, 0, 2, 1), (SEND, 0, 2, 9, 0),
    (SEND, 1, 4, 6, 0), (SEND, 1, 0, 5, 1), (ARRIVE, 0, 3, 2), (ARRIVE, 0, 1, 2), (ARRIVE, 0, 5, 2),
    (ARRIVE, 1, 0, 2), (ARRIVE, 1, 4, 2), (ARRIVE, 0, 2, 3), (SEND, 0, 1, 4, 2), (SEND, 1, 0, 3, 2),
    (SEND, 1, 0, 2, 2), (SEND, 1, 0, 5, 2), (SEND, 0, 0, 1, 6), (SEND, 1, 1, 0, 6), (ARRIVE, 0, 3, 3),
    (ARRIVE, 0, 1, 3), (ARRIVE, 0, 5, 3), (ARRIVE, 1, 0, 3), (ARRIVE, 1, 4, 3), (ARRIVE, 0, 2, 4),
    (SEND, 0, 1, 4, 3), (SEND, 1, 0, 3, 3), (SEND, 1, 0, 2, 3), (BEGIN, 0), (BEGIN, 1), (SEND, 0, 5, 7, 3),
    (ARRIVE, 0, 4, 0), (ARRIVE, 1, 3, 0), (ARRIVE, 1, 5, 0), (ARRIVE, 1, 2, 0), (ARRIVE, 0, 1, 4), (ARRIVE, 1, 0, 4),
    (SEND, 0, 4, 6, 0), (SEND, 1, 2, 9, 0), (SEND, 0, 1, 4, 4), (SEND, 1, 0, 3, 4), (SEND, 1, 0, 2, 4),
    (SEND, 1, 4, 6, 1), (SEND, 0, 0, 3, 4), (SEND, 1, 1, 4, 4), (ARRIVE, 0, 4, 1), (ARRIVE, 0, 7, 1),
    (ARRIVE, 1, 3, 1), (ARRIVE, 1, 2, 1), (ARRIVE, 0, 1, 5), (ARRIVE, 1, 0, 5), (SEND, 0, 7, 2, 1),
    (SEND, 1, 2, 9, 1), (SEND, 1, 0, 2, 5), (SEND, 0, 4, 6, 1), (SEND, 0, 7, 8, 1), (SEND, 1, 0, 5, 3),
    (SEND, 0, 0, 2, 5), (SEND, 0, 1, 4, 5), (SEND, 1, 0, 3, 5), (ARRIVE, 0, 9, 0), (ARRIVE, 1, 6, 0),
    (ARRIVE, 1, 5, 1), (ARRIVE, 0, 4, 2), (ARRIVE, 1, 3, 2), (ARRIVE, 1, 2, 2), (SEND, 0, 4, 6, 2),
    (SEND, 0, 0, 3, 5), (SEND, 1, 1, 4, 5), (ARRIVE, 1, 5, 2), (ARRIVE, 0, 4, 3), (ARRIVE, 1, 3, 3),
    (ARRIVE, 1, 2, 3), (ARRIVE, 0, 1, 6), (ARRIVE, 1, 0, 6), (SEND, 1, 5, 7, 2), (SEND, 1, 2, 9, 3),
    (SEND, 1, 0, 2, 6), (BEGIN, 2), (BEGIN, 3), (BEGIN, 4), (SEND, 1, 4, 6, 2), (SEND, 0, 2, 9, 3),
    (SEND, 1, 0, 5, 4), (SEND, 0, 0, 3, 6), (SEND, 0, 0, 2, 6), (SEND, 1, 1, 4, 6), (READY, 0), (READY, 1),
    (ARRIVE, 0, 6, 0), (ARRIVE, 1, 9, 0), (ARRIVE, 0, 7, 3), (ARRIVE, 0, 4, 4), (ARRIVE, 1, 3, 4), (ARRIVE, 1, 2, 4),
    (BEGIN, 5), (SEND, 1, 2, 7, 0), (SEND, 1, 4, 6, 3), (SEND, 0, 0, 5, 4), (SEND, 0, 1, 4, 6), (SEND, 1, 0, 3, 6),
    (OWN, 0), (ARRIVE, 0, 2, 1), (ARRIVE, 1, 9, 1), (ARRIVE, 1, 6, 1), (ARRIVE, 0, 3, 4), (ARRIVE, 1, 4, 4),
    (ARRIVE, 1, 2, 5), (SEND, 0, 2, 9, 1), (SEND, 0, 3, 10, 0), (SEND, 1, 6, 11, 0), (SEND, 1, 2, 7, 1),
    (SEND, 0, 4, 6, 3), (SEND, 1, 2, 9, 4), (SEND, 0, 0, 5, 5), (PAIRS, 1, (0,)), (ARRIVE, 0, 6, 1),
    (ARRIVE, 0, 8, 1), (ARRIVE, 1, 5, 3), (ARRIVE, 0, 2, 5), (ARRIVE, 0, 4, 5), (ARRIVE, 1, 3, 5),
    (SEND, 0, 6, 11, 0), (SEND, 1, 3, 10, 0), (SEND, 0, 2, 7, 2), (SEND, 1, 4, 6, 4), (SEND, 1, 0, 5, 5),
    (ARRIVE, 0, 6, 2), (ARRIVE, 1, 7, 2), (ARRIVE, 1, 9, 3), (ARRIVE, 0, 3, 5), (ARRIVE, 1, 4, 5), (ARRIVE, 1, 2, 6),
    (SEND, 1, 7, 8, 2), (SEND, 0, 3, 10, 1), (SEND, 1, 6, 11, 1), (SEND, 1, 2, 7, 3), (SEND, 0, 4, 6, 4),
    (SEND, 1, 2, 9, 5), (SEND, 0, 0, 5, 6), (ARRIVE, 1, 6, 2), (ARRIVE, 0, 9, 3), (ARRIVE, 1, 5, 4),
    (ARRIVE, 0, 3, 6), (ARRIVE, 0, 2, 6), (ARRIVE, 1, 4, 6), (SEND, 1, 9, 8, 0), (SEND, 0, 6, 11, 1),
    (SEND, 1, 3, 10, 1), (SEND, 1, 4, 6, 5), (SEND, 0, 2, 9, 6), (SEND, 1, 0, 5, 6), (READY, 2), (PAIRS, 2, (0, 1)),
    (ARRIVE, 1, 7, 0), (ARRIVE, 0, 9, 1), (ARRIVE, 1, 6, 3), (ARRIVE, 0, 5, 4), (ARRIVE, 0, 4, 6), (ARRIVE, 1, 3, 6),
    (BEGIN, 6), (SEND, 0, 9, 8, 0), (SEND, 0, 6, 11, 2), (SEND, 1, 3, 10, 2), (SEND, 0, 4, 6, 5), (READY, 3),
    (READY, 4), (ARRIVE, 0, 10, 0), (ARRIVE, 1, 11, 0), (ARRIVE, 1, 7, 1), (ARRIVE, 0, 6, 3), (ARRIVE, 1, 9, 4),
    (ARRIVE, 0, 5, 5), (SEND, 1, 7, 8, 1), (SEND, 0, 5, 7, 5), (SEND, 0, 3, 10, 2), (SEND, 1, 6, 11, 2),
    (SEND, 0, 2, 7, 4), (SEND, 0, 4, 6, 6), (PAIRS, 4, (0, 1, 2)), (ARRIVE, 0, 11, 0), (ARRIVE, 1, 10, 0),
    (ARRIVE, 0, 7, 2), (ARRIVE, 1, 8, 2), (ARRIVE, 1, 6, 4), (ARRIVE, 1, 5, 5), (SEND, 0, 7, 8, 2),
    (SEND, 1, 8, 9, 2), (SEND, 0, 3, 10, 3), (SEND, 1, 6, 11, 3), (SEND, 1, 2, 7, 4), (SEND, 1, 2, 9, 6),
    (SEND, 1, 4, 6, 6), (ARRIVE, 0, 10, 1), (ARRIVE, 1, 11, 1), (ARRIVE, 1, 7, 3), (ARRIVE, 0, 6, 4),
    (ARRIVE, 1, 9, 5), (ARRIVE, 0, 5, 6), (SEND, 0, 5, 7, 6), (BEGIN, 7), (SEND, 0, 6, 11, 3), (SEND, 1, 3, 10, 3),
    (SEND, 1, 2, 7, 5), (PAIRS, 3, (2, 4)), (ARRIVE, 1, 8, 0), (ARRIVE, 0, 11, 1), (ARRIVE, 1, 10, 1),
    (ARRIVE, 1, 6, 5), (ARRIVE, 0, 9, 6), (ARRIVE, 1, 5, 6), (SEND, 1, 5, 7, 6), (SEND, 0, 9, 8, 3),
    (SEND, 0, 3, 10, 4), (SEND, 1, 6, 11, 4), (READY, 5), (ARRIVE, 0, 8, 0), (ARRIVE, 1, 8, 1), (ARRIVE, 0, 11, 2),
    (ARRIVE, 1, 10, 2), (ARRIVE, 0, 7, 5), (ARRIVE, 0, 6, 5), (SEND, 0, 8, 7, 0), (SEND, 0, 7, 8, 5),
    (SEND, 1, 9, 8, 3), (SEND, 0, 6, 11, 4), (SEND, 1, 3, 10, 4), (PAIRS, 5, (1, 3, 4)), (ARRIVE, 0, 10, 2),
    (ARRIVE, 0, 8, 2), (ARRIVE, 1, 9, 2), (ARRIVE, 1, 11, 2), (ARRIVE, 0, 7, 4), (ARRIVE, 0, 6, 6),
    (SEND, 0, 8, 9, 2), (SEND, 0, 7, 8, 4), (SEND, 1, 9, 8, 4), (SEND, 0, 3, 10, 5), (SEND, 1, 6, 11, 5),
    (ARRIVE, 0, 10, 3), (ARRIVE, 1, 11, 3), (ARRIVE, 1, 7, 4), (ARRIVE, 0, 7, 6), (ARRIVE, 1, 9, 6),
    (ARRIVE, 1, 6, 6), (SEND, 0, 7, 8, 6), (BEGIN, 8), (BEGIN, 10), (BEGIN, 11), (SEND, 0, 6, 11, 5),
    (SEND, 1, 3, 10, 5), (SEND, 1, 9, 8, 6), (READY, 6), (ARRIVE, 0, 11, 3), (ARRIVE, 1, 10, 3), (ARRIVE, 1, 7, 5),
    (ARRIVE, 1, 7, 6), (SEND, 1, 7, 8, 5), (SEND, 0, 3, 10, 6), (SEND, 1, 6, 11, 6), (PAIRS, 6, (0, 2, 5)),
    (FOLD, (5,)), (ARRIVE, 0, 7, 0), (ARRIVE, 0, 8, 5), (SEND, 0, 8, 9, 5), (ARRIVE, 0, 8, 3), (ARRIVE, 0, 10, 4),
    (ARRIVE, 1, 11, 4), (SEND, 0, 6, 11, 6), (SEND, 1, 3, 10, 6), (READY, 7), (ARRIVE, 0, 9, 2), (ARRIVE, 0, 8, 4),
    (SEND, 0, 8, 9, 4), (ARRIVE, 1, 8, 3), (ARRIVE, 0, 11, 4), (ARRIVE, 1, 10, 4), (PAIRS, 7, (1, 3, 4)),
    (ARRIVE, 0, 8, 6), (BEGIN, 9), (ARRIVE, 1, 8, 4), (ARRIVE, 0, 10, 5), (ARRIVE, 1, 11, 5), (ARRIVE, 1, 8, 5),
    (PAIRS, 7, (6,)), (ARRIVE, 0, 11, 5), (ARRIVE, 1, 10, 5), (ARRIVE, 1, 8, 6), (ARRIVE, 0, 9, 5),
    (SHARED, 7, (0,), 2), (READY, 8), (ARRIVE, 0, 10, 6), (ARRIVE, 1, 11, 6), (PAIRS, 8, (3,)), (ARRIVE, 0, 9, 4),
    (SHARED, 8, (1,), 1), (ARRIVE, 0, 11, 6), (ARRIVE, 1, 10, 6), (SHARED, 6, (3,), 0), (READY, 9),
    (PAIRS, 9, (1, 3, 6)), (FOLD, (1, 3, 6)), (READY, 10), (READY, 11), (PAIRS, 11, (2, 8, 9)), (FOLD, (8,)),
    (SHARED, 11, (10, 7), 1), (FOLD, (11,)), (PAIRS, 10, (2, 4, 9)), (FOLD, (2, 4, 9)), (SHARED, 10, (7, 0), 0),
    (FOLD, (0, 7, 10)),
)

ROWS = 448
WINDOW = 128
CLUSTERS = 8
NONE = 1 << 20


def place():
    row, grp = lax.axis_index("row"), lax.axis_index("grp")
    return grp // 4, row // 2, grp % 4, row % 2


def device(x, y, z, core):
    return (lax.rem(y + 4, 4) * 2 + core, lax.rem(x + 4, 4) * 4 + lax.rem(z + 4, 4))


def scores(left, right):
    return lax.dot_general(
        left, right, (((1,), (1,)), ((), ())), preferred_element_type=jnp.float32
    )


def kernel(emb, scales, cid, rank, out, *refs):
    own, sib = refs[:SLOTS], refs[SLOTS : 2 * SLOTS]
    (
        unit, table, meta_own, meta_sib, first_own, first_sib, col, row_best, col_best, outgoing, incoming,
        recv, recv_meta, sib_recv, sib_recv_meta, sent, sent_meta, sib_sent, sib_sent_meta, local, back_sent, back_recv,
    ) = refs[2 * SLOTS :]
    x, y, z, core = place()
    root = ROOTS[0] + core * (ROOTS[1] - ROOTS[0])
    chunk_rows = ROWS // CHUNKS
    def other():
        return device(x, y, z, 1 - core)

    barrier = pltpu.get_barrier_semaphore()
    for dx, dy, dz in ((1, 0, 0), (-1, 0, 0), (0, 1, 0), (0, -1, 0), (0, 0, 1), (0, 0, -1)):
        pl.semaphore_signal(
            barrier, inc=1, device_id=device(x + dx, y + dy, z + dz, core), device_id_type=MESH
        )
    pl.semaphore_signal(barrier, inc=1, device_id=other(), device_id_type=MESH)

    def clear(i, _):
        row_best[i] = jnp.full((2 * WINDOW, WINDOW), -1.0, jnp.float32)
        col_best[i] = jnp.full((8, 2 * WINDOW), -1.0, jnp.float32)
        return 0

    lax.fori_loop(0, SLOTS * 4, clear, 0)

    factor = scales[...].T
    total = jnp.zeros((ROWS, 1), jnp.float32)
    for b in range(8):
        part = emb[:, b * 128 : (b + 1) * 128].astype(jnp.float32) * factor[:, b : b + 1]
        total = total + jnp.sum(part * part, axis=1, keepdims=True)
    inverse = lax.rsqrt(total + 1e-06)
    for b in range(8):
        part = emb[:, b * 128 : (b + 1) * 128].astype(jnp.float32) * factor[:, b : b + 1]
        unit[:, b * 128 : (b + 1) * 128] = (part * inverse).astype(jnp.bfloat16)

    cids, ranks = cid[...], rank[...]
    sub16 = lax.broadcasted_iota(jnp.int32, (16, ROWS), 0)
    member = sub16 == cids
    earlier = (
        lax.broadcasted_iota(jnp.int32, (ROWS, ROWS), 0) < lax.broadcasted_iota(jnp.int32, (ROWS, ROWS), 1)
    )
    before = jnp.dot(
        jnp.where(member, 1.0, 0.0).astype(jnp.bfloat16),
        jnp.where(earlier, 1.0, 0.0).astype(jnp.bfloat16),
        preferred_element_type=jnp.float32,
    )
    sub128 = lax.broadcasted_iota(jnp.int32, (WINDOW, ROWS), 0)
    start = jnp.sum(jnp.where(cids < sub128, 1, 0), axis=1, keepdims=True)
    position = jnp.sum(
        jnp.where(member, before + start[0:16].astype(jnp.float32), 0.0), axis=0, keepdims=True
    ).astype(jnp.int32)
    tile_start = jnp.minimum(start >> 4, (ROWS - WINDOW) // 16)
    window_start = tile_start * 16
    diagonal = lax.broadcasted_iota(jnp.int32, (WINDOW, WINDOW), 0) == lax.broadcasted_iota(
        jnp.int32, (WINDOW, WINDOW), 1
    )
    start_row = jnp.sum(jnp.where(diagonal, tile_start, 0), axis=0, keepdims=True)
    def make_table():
        for c in range(CLUSTERS):
            spot = window_start[c : c + 1, :] + lax.broadcasted_iota(jnp.int32, (WINDOW, ROWS), 0)
            hit = jnp.logical_and(spot == position, cids == c)
            table[c * WINDOW : (c + 1) * WINDOW, :] = jnp.where(hit, 1.0, 0.0).astype(jnp.bfloat16)
        digits = jnp.where(
            sub16 == 0, ranks >> 7, jnp.where(sub16 == 1, ranks & 127, jnp.where(sub16 == 2, 1, 0))
        ).astype(jnp.float32).astype(jnp.bfloat16)
        placed = scores(digits, table[...])
        slot_rank = jnp.where(placed[2:3] > 0.5, placed[0:1] * 128.0 + placed[1:2], float(NONE)).astype(jnp.int32)
        meta_own[root] = jnp.concatenate(
            [slot_rank[:, c * WINDOW : (c + 1) * WINDOW] for c in range(CLUSTERS)]
            + [start_row, jnp.zeros((7, WINDOW), jnp.int32)],
            axis=0,
        )

    def sort_chunk(k):
        spot = lax.broadcasted_iota(jnp.int32, (chunk_rows, ROWS), 0) + k * chunk_rows
        move = jnp.where(spot == position, 1.0, 0.0).astype(jnp.bfloat16)
        rows = jnp.dot(move, unit[...], preferred_element_type=jnp.float32).astype(jnp.bfloat16)
        for c in (0, 1):

            @pl.when(core == c)
            def _():
                own[ROOTS[c]][k * chunk_rows : (k + 1) * chunk_rows, :] = rows

    def piece(ref, chunk):
        return ref.at[pl.ds(chunk * chunk_rows, chunk_rows)]

    def to_sibling(slot, chunk):
        return pltpu.make_async_remote_copy(
            src_ref=own[slot] if chunk is None else piece(own[slot], chunk),
            dst_ref=sib[slot] if chunk is None else piece(sib[slot], chunk),
            send_sem=sib_sent.at[slot], recv_sem=sib_recv.at[slot],
            device_id=other(), device_id_type=MESH,
        )

    def meta_to_sibling(slot):
        return pltpu.make_async_remote_copy(
            src_ref=meta_own.at[slot], dst_ref=meta_sib.at[slot],
            send_sem=sib_sent_meta.at[slot], recv_sem=sib_recv_meta.at[slot],
            device_id=other(), device_id_type=MESH,
        )

    def target(e, d):
        ux, uy, uz = (q - p for p, q in zip(OFFSETS[e], OFFSETS[d]))
        return device(x - ux, y - uy, z - uz, core)

    def along(e, d, chunk):
        return pltpu.make_async_remote_copy(
            src_ref=own[e] if chunk is None else piece(own[e], chunk),
            dst_ref=own[d] if chunk is None else piece(own[d], chunk),
            send_sem=sent.at[d],
            recv_sem=recv.at[d * CHUNKS + (chunk or 0)],
            device_id=target(e, d), device_id_type=MESH,
        )

    def meta_along(e, d):
        return pltpu.make_async_remote_copy(
            src_ref=meta_own.at[e], dst_ref=meta_own.at[d],
            send_sem=sent_meta.at[d], recv_sem=recv_meta.at[d],
            device_id=target(e, d), device_id_type=MESH,
        )

    def starts_to_scalars(slot):
        return [
            pltpu.make_async_copy(meta.at[slot, pl.ds(8, 1)], first.at[slot], local.at[slot * 2 + n])
            for n, (meta, first) in enumerate(((meta_own, first_own), (meta_sib, first_sib)))
        ]

    def arrive(c, slot, chunk):
        if slot != ROOTS[c]:
            e = parent_of[(c, slot, chunk)]
            along(e, slot, chunk).wait_recv()
            if chunk == EXTRA:
                meta_along(e, slot).wait_recv()
        if chunk == EXTRA:
            meta_to_sibling(slot).start()
        to_sibling(slot, chunk).start()

    def send(c, e, d, chunk):
        if chunk == EXTRA:
            meta_along(e, d).start()
        along(e, d, chunk).start()

    parent_of = {}
    for item in PLAN:
        if item[0] == SEND:
            _, c, e, d, chunk = item
            parent_of[(c, d, chunk)] = e

    def begin(slot):
        meta_to_sibling(slot).wait_recv()
        for copy in starts_to_scalars(slot):
            copy.start()
        for n, meta in enumerate((meta_own, meta_sib)):
            tile = meta[slot, 0:8, :]
            mine = jnp.where(core == 0, tile, jnp.concatenate([tile[4:8], tile[0:4]], axis=0))
            turned = mine.astype(jnp.float32).T
            for q in range(4):
                col[slot * 4 + q, pl.ds(n * WINDOW, WINDOW), :] = jnp.broadcast_to(
                    turned[:, q : q + 1], (WINDOW, WINDOW)
                )

    def ready(slot):
        to_sibling(slot, None).wait_recv()
        for copy in starts_to_scalars(slot):
            copy.wait()

    def window(slot, cluster):
        return [
            ref[pl.ds(first[slot, 0, cluster] * 16, WINDOW), :]
            for ref, first in ((own[slot], first_own), (sib[slot], first_sib))
        ]

    def pairs(b, group, count, base, itself=False):
        def one(i, _):
            q = base + i
            cluster = core * 4 + q
            right = jnp.concatenate(window(b, cluster), axis=0)
            left = jnp.concatenate([w for a in group for w in window(a, cluster)], axis=0)
            found = scores(left, right)
            right_rank = jnp.concatenate(
                [meta[b, pl.ds(cluster, 1), :] for meta in (meta_own, meta_sib)], axis=1
            ).astype(jnp.float32)
            for n, a in enumerate(group):
                value = found[n * 2 * WINDOW : (n + 1) * 2 * WINDOW]
                less = right_rank < jnp.concatenate([col[a * 4 + q]] * 2, axis=1)
                to_left = jnp.where(less, value, -1.0)
                row_best[a * 4 + q] = jnp.maximum(
                    row_best[a * 4 + q], jnp.maximum(to_left[:, :WINDOW], to_left[:, WINDOW:])
                )
                if not itself:
                    to_right = jnp.where(less, -1.0, value).reshape(2 * WINDOW // 8, 8, 2 * WINDOW)
                    col_best[b * 4 + q] = jnp.maximum(col_best[b * 4 + q], jnp.max(to_right, axis=0))
            return 0

        lax.fori_loop(0, count, one, 0, unroll=4)

    def on_core(c, steps):
        @pl.when(core == c)
        def _():
            for step in steps:
                step()

    def sent_to(d):
        along((d + 1) % SLOTS, d, None).wait_send()
        meta_along((d + 1) % SLOTS, d).wait_send()

    def reply(d, n):
        away = [[q - p for p, q in zip(OFFSETS[ROOTS[c]], OFFSETS[d])] for c in (n, 1 - n)]
        ox, oy, oz = (first + core * (second - first) for first, second in zip(*away))
        return pltpu.make_async_remote_copy(
            src_ref=outgoing.at[n * SLOTS + d], dst_ref=incoming.at[n * SLOTS + d],
            send_sem=back_sent.at[d * 2 + n], recv_sem=back_recv.at[d * 2 + n],
            device_id=device(x + ox, y + oy, z + oz, core if n == 0 else 1 - core), device_id_type=MESH,
        )

    def replies(d, what):
        if d not in ROOTS:
            getattr(reply(d, 0), what)()
        elif ROOTS[0] != ROOTS[1]:
            on_core(1 - ROOTS.index(d), [getattr(reply(d, 0), what)])
        getattr(reply(d, 1), what)()

    lane = lax.broadcasted_iota(jnp.int32, (2 * WINDOW, WINDOW), 1)

    def fold(group):
        best = jnp.full((2 * WINDOW, WINDOW), -1.0, jnp.float32)
        for n, d in enumerate(group):
            for q in range(4):
                best = jnp.where(lane == n * 8 + q, jnp.max(row_best[d * 4 + q], axis=1, keepdims=True), best)
        turned = best.T
        for n, d in enumerate(group):
            rows = jnp.concatenate(
                [jnp.max(col_best[d * 4 + q], axis=0, keepdims=True) for q in range(4)]
                + [jnp.full((4, 2 * WINDOW), -1.0, jnp.float32)],
                axis=0,
            )
            rows = jnp.maximum(rows, turned[n * 8 : (n + 1) * 8])
            for half in (0, 1):
                outgoing[half * SLOTS + d] = rows[:, half * WINDOW : (half + 1) * WINDOW]
            replies(d, "start")

    pending = [[], []]

    def flush():
        for c in (0, 1):
            if pending[c]:
                on_core(c, pending[c])
            pending[c] = []

    pl.semaphore_wait(barrier, 7)
    for item in PLAN:
        if item[0] == ARRIVE:
            pending[item[1]].append(functools.partial(arrive, *item[1:]))
            continue
        if item[0] == SEND:
            pending[item[1]].append(functools.partial(send, *item[1:]))
            continue
        flush()
        if item[0] == SORT:
            sort_chunk(item[1])
        elif item[0] == TABLE:
            make_table()
        elif item[0] == BEGIN:
            begin(item[1])
        elif item[0] == READY:
            ready(item[1])
        elif item[0] == PAIRS:
            pairs(item[1], item[2], 4, 0)
        elif item[0] == SHARED:
            pairs(item[1], item[2], 2, (x, y, z)[item[3]] // 2 * 2)
        elif item[0] == FOLD:
            fold(item[1])
        else:
            pairs(item[1], (item[1],), 4, 0, itself=True)
    flush()

    for d in range(SLOTS):
        to_sibling(d, None).wait_send()
        meta_to_sibling(d).wait_send()
        if d not in ROOTS:
            sent_to(d)
        elif ROOTS[0] != ROOTS[1]:
            on_core(1 - ROOTS.index(d), [functools.partial(sent_to, d)])
    for what in ("wait_send", "wait_recv"):
        for d in range(SLOTS):
            replies(d, what)
    incoming[root] = outgoing[root]
    final = []
    for n in (0, 1):
        best = incoming[n * SLOTS]
        for d in range(1, SLOTS):
            best = jnp.maximum(best, incoming[n * SLOTS + d])
        final.append(best)
    lower = jnp.where(core == 0, final[0], final[1])
    upper = jnp.where(core == 0, final[1], final[0])
    line = jnp.concatenate([lower[q : q + 1] for q in range(4)] + [upper[q : q + 1] for q in range(4)], axis=1)
    high = line.astype(jnp.bfloat16)
    rest = line - high.astype(jnp.float32)
    middle = rest.astype(jnp.bfloat16)
    low = (rest - middle.astype(jnp.float32)).astype(jnp.bfloat16)
    sub = lax.broadcasted_iota(jnp.int32, (16, CLUSTERS * WINDOW), 0)
    parts = jnp.where(
        sub == 0, high.astype(jnp.float32),
        jnp.where(sub == 1, middle.astype(jnp.float32), jnp.where(sub == 2, low.astype(jnp.float32), 0.0)),
    ).astype(jnp.bfloat16)
    out[...] = jnp.sum(jnp.dot(parts, table[...], preferred_element_type=jnp.float32), axis=0, keepdims=True)


def local(embeddings, scales, cluster_id, doc_rank):
    vmem = pl.BlockSpec(memory_space=pltpu.VMEM)
    dma = pltpu.SemaphoreType.DMA
    best = pl.pallas_call(
        kernel,
        out_shape=jax.ShapeDtypeStruct((1, ROWS), jnp.float32),
        in_specs=[vmem] * 4,
        out_specs=vmem,
        scratch_shapes=[pltpu.VMEM((ROWS, 1024), jnp.bfloat16)] * (2 * SLOTS)
        + [
            pltpu.VMEM((ROWS, 1024), jnp.bfloat16),
            pltpu.VMEM((CLUSTERS * WINDOW, ROWS), jnp.bfloat16),
            pltpu.VMEM((SLOTS, 16, WINDOW), jnp.int32),
            pltpu.VMEM((SLOTS, 16, WINDOW), jnp.int32),
            pltpu.SMEM((SLOTS, 1, WINDOW), jnp.int32),
            pltpu.SMEM((SLOTS, 1, WINDOW), jnp.int32),
            pltpu.VMEM((SLOTS * 4, 2 * WINDOW, WINDOW), jnp.float32),
            pltpu.VMEM((SLOTS * 4, 2 * WINDOW, WINDOW), jnp.float32),
            pltpu.VMEM((SLOTS * 4, 8, 2 * WINDOW), jnp.float32),
            pltpu.VMEM((2 * SLOTS, 8, WINDOW), jnp.float32),
            pltpu.VMEM((2 * SLOTS, 8, WINDOW), jnp.float32),
            dma((SLOTS * CHUNKS,)),
            dma((SLOTS,)),
            dma((SLOTS,)),
            dma((SLOTS,)),
            dma((SLOTS,)),
            dma((SLOTS,)),
            dma((SLOTS,)),
            dma((SLOTS,)),
            dma((2 * SLOTS,)),
            dma((2 * SLOTS,)),
            dma((2 * SLOTS,)),
        ],
        compiler_params=pltpu.CompilerParams(
            collective_id=0, has_side_effects=True, vmem_limit_bytes=56 * 2**20
        ),
        cost_estimate=pl.CostEstimate(flops=30 * 10**9, bytes_accessed=2**20, transcendentals=0),
        name="nearest_in_cluster",
    )(embeddings, scales.T, cluster_id.reshape(1, ROWS), doc_rank.reshape(1, ROWS))
    return best.reshape(ROWS)


def solution(mesh):
    return jax.shard_map(
        local,
        mesh=mesh,
        in_specs=(P(("row", "grp"), None), P(("row", "grp"), None), P(("row", "grp")), P(("row", "grp"))),
        out_specs=P(("row", "grp")),
        check_vma=False,
    )
```

```python
import functools

import jax
import jax.numpy as jnp
from jax import lax
from jax.experimental import pallas as pl
from jax.experimental.pallas import tpu as pltpu
from jax.sharding import PartitionSpec as P

MESH = pl.DeviceIdType.MESH

OFFSETS = (
    (0, 0, 0), (0, 1, 0), (0, 0, 3), (1, 0, 0), (3, 1, 0), (0, 0, 1), (3, 2, 0), (0, 0, 2), (0, 3, 2), (0, 3, 3),
    (2, 0, 0), (2, 2, 0),
)
SLOTS = len(OFFSETS)
ROOTS = (0, 1)
EXTRA = 1
CHUNKS = 7
SORT, ARRIVE, SEND, BEGIN, READY, PAIRS, SHARED, OWN, TABLE, FOLD = range(10)
PLAN = (
    (SORT, 0), (TABLE,), (ARRIVE, 0, 0, 0), (ARRIVE, 1, 1, 0), (SEND, 0, 0, 3, 0), (SEND, 0, 0, 1, 0),
    (SEND, 0, 0, 5, 0), (SEND, 0, 0, 2, 0), (SEND, 1, 1, 0, 0), (SEND, 1, 1, 4, 0), (SORT, 1), (SORT, 2),
    (ARRIVE, 0, 0, 1), (ARRIVE, 1, 1, 1), (SEND, 0, 0, 3, 1), (SEND, 0, 0, 1, 1), (SEND, 0, 0, 5, 1),
    (SEND, 1, 1, 0, 1), (SEND, 1, 1, 4, 1), (SORT, 3), (ARRIVE, 0, 0, 2), (ARRIVE, 1, 1, 2), (SEND, 0, 0, 3, 2),
    (SEND, 0, 0, 1, 2), (SEND, 0, 0, 5, 2), (SEND, 0, 0, 2, 2), (SEND, 1, 1, 0, 2), (SEND, 1, 1, 4, 2), (SORT, 4),
    (ARRIVE, 0, 0, 3), (ARRIVE, 1, 1, 3), (SEND, 0, 0, 2, 3), (SORT, 5), (ARRIVE, 0, 0, 4), (ARRIVE, 1, 1, 4),
    (SORT, 6), (ARRIVE, 0, 0, 5), (ARRIVE, 1, 1, 5), (SEND, 0, 0, 3, 3), (SEND, 0, 0, 1, 3), (SEND, 0, 0, 5, 3),
    (SEND, 1, 1, 0, 3), (SEND, 1, 1, 4, 3), (SEND, 0, 0, 2, 4), (ARRIVE, 0, 0, 6), (ARRIVE, 1, 1, 6),
    (SEND, 0, 0, 1, 4), (SEND, 1, 1, 0, 4), (ARRIVE, 0, 3, 0), (ARRIVE, 0, 1, 0), (ARRIVE, 0, 5, 0),
    (ARRIVE, 0, 2, 0), (ARRIVE, 1, 0, 0), (ARRIVE, 1, 4, 0), (SEND, 0, 1, 4, 0), (SEND, 1, 0, 3, 0),
    (SEND, 1, 0, 5, 0), (SEND, 1, 0, 2, 0), (SEND, 0, 0, 1, 5), (SEND, 1, 1, 0, 5), (ARRIVE, 0, 3, 1),
    (ARRIVE, 0, 1, 1), (ARRIVE, 0, 5, 1), (ARRIVE, 1, 0, 1), (ARRIVE, 1, 4, 1), (ARRIVE, 0, 2, 2),
    (SEND, 0, 1, 4, 1), (SEND, 0, 5, 7, 1), (SEND, 1, 0, 3, 1), (SEND, 1, 0, 2, 1), (SEND, 0, 2, 9, 0),
    (SEND, 1, 4, 6, 0), (SEND, 1, 0, 5, 1), (ARRIVE, 0, 3, 2), (ARRIVE, 0, 1, 2), (ARRIVE, 0, 5, 2),
    (ARRIVE, 1, 0, 2), (ARRIVE, 1, 4, 2), (ARRIVE, 0, 2, 3), (SEND, 0, 1, 4, 2), (SEND, 1, 0, 3, 2),
    (SEND, 1, 0, 2, 2), (BEGIN, 0), (BEGIN, 1), (SEND, 1, 0, 5, 2), (SEND, 0, 0, 1, 6), (SEND, 1, 1, 0, 6),
    (ARRIVE, 0, 3, 3), (ARRIVE, 0, 1, 3), (ARRIVE, 0, 5, 3), (ARRIVE, 1, 0, 3), (ARRIVE, 1, 4, 3), (ARRIVE, 0, 2, 4),
    (SEND, 0, 1, 4, 3), (SEND, 1, 0, 3, 3), (SEND, 1, 0, 2, 3), (SEND, 0, 5, 7, 3), (ARRIVE, 0, 4, 0),
    (ARRIVE, 1, 3, 0), (ARRIVE, 1, 5, 0), (ARRIVE, 1, 2, 0), (ARRIVE, 0, 1, 4), (ARRIVE, 1, 0, 4),
    (SEND, 0, 4, 6, 0), (SEND, 1, 2, 9, 0), (SEND, 0, 1, 4, 4), (SEND, 1, 0, 3, 4), (SEND, 1, 0, 2, 4),
    (SEND, 1, 4, 6, 1), (SEND, 0, 0, 3, 4), (SEND, 1, 1, 4, 4), (ARRIVE, 0, 4, 1), (ARRIVE, 0, 7, 1),
    (ARRIVE, 1, 3, 1), (ARRIVE, 1, 2, 1), (ARRIVE, 0, 1, 5), (ARRIVE, 1, 0, 5), (SEND, 0, 7, 2, 1),
    (SEND, 1, 2, 9, 1), (SEND, 1, 0, 2, 5), (SEND, 0, 4, 6, 1), (SEND, 0, 7, 8, 1), (SEND, 1, 0, 5, 3),
    (SEND, 0, 0, 2, 5), (SEND, 0, 1, 4, 5), (SEND, 1, 0, 3, 5), (ARRIVE, 0, 9, 0), (ARRIVE, 1, 6, 0),
    (ARRIVE, 1, 5, 1), (ARRIVE, 0, 4, 2), (ARRIVE, 1, 3, 2), (ARRIVE, 1, 2, 2), (BEGIN, 3), (BEGIN, 4),
    (SEND, 0, 4, 6, 2), (SEND, 0, 0, 3, 5), (SEND, 1, 1, 4, 5), (ARRIVE, 1, 5, 2), (ARRIVE, 0, 4, 3),
    (ARRIVE, 1, 3, 3), (ARRIVE, 1, 2, 3), (ARRIVE, 0, 1, 6), (ARRIVE, 1, 0, 6), (SEND, 1, 5, 7, 2),
    (SEND, 1, 2, 9, 3), (SEND, 1, 0, 2, 6), (BEGIN, 5), (SEND, 1, 4, 6, 2), (SEND, 0, 2, 9, 3), (SEND, 1, 0, 5, 4),
    (SEND, 0, 0, 3, 6), (SEND, 0, 0, 2, 6), (SEND, 1, 1, 4, 6), (READY, 0), (READY, 1), (ARRIVE, 0, 6, 0),
    (ARRIVE, 1, 9, 0), (ARRIVE, 0, 7, 3), (ARRIVE, 0, 4, 4), (ARRIVE, 1, 3, 4), (ARRIVE, 1, 2, 4),
    (SEND, 1, 2, 7, 0), (SEND, 1, 4, 6, 3), (SEND, 0, 0, 5, 4), (SEND, 0, 1, 4, 6), (SEND, 1, 0, 3, 6), (OWN, 0),
    (PAIRS, 1, (0,)), (ARRIVE, 0, 2, 1), (ARRIVE, 1, 9, 1), (ARRIVE, 1, 6, 1), (ARRIVE, 0, 3, 4), (ARRIVE, 1, 4, 4),
    (ARRIVE, 1, 2, 5), (SEND, 0, 2, 9, 1), (SEND, 0, 3, 10, 0), (SEND, 1, 6, 11, 0), (SEND, 1, 2, 7, 1),
    (SEND, 0, 4, 6, 3), (SEND, 1, 2, 9, 4), (SEND, 0, 0, 5, 5), (ARRIVE, 0, 6, 1), (ARRIVE, 0, 8, 1),
    (ARRIVE, 1, 5, 3), (ARRIVE, 0, 2, 5), (ARRIVE, 0, 4, 5), (ARRIVE, 1, 3, 5), (BEGIN, 2), (SEND, 0, 6, 11, 0),
    (SEND, 1, 3, 10, 0), (SEND, 0, 2, 7, 2), (SEND, 1, 4, 6, 4), (SEND, 1, 0, 5, 5), (ARRIVE, 0, 6, 2),
    (ARRIVE, 1, 7, 2), (ARRIVE, 1, 9, 3), (ARRIVE, 0, 3, 5), (ARRIVE, 1, 4, 5), (ARRIVE, 1, 2, 6),
    (SEND, 1, 7, 8, 2), (BEGIN, 6), (SEND, 0, 3, 10, 1), (SEND, 1, 6, 11, 1), (SEND, 1, 2, 7, 3), (SEND, 0, 4, 6, 4),
    (SEND, 1, 2, 9, 5), (SEND, 0, 0, 5, 6), (ARRIVE, 1, 6, 2), (ARRIVE, 0, 9, 3), (ARRIVE, 1, 5, 4),
    (ARRIVE, 0, 3, 6), (ARRIVE, 0, 2, 6), (ARRIVE, 1, 4, 6), (SEND, 1, 9, 8, 0), (SEND, 0, 6, 11, 1),
    (SEND, 1, 3, 10, 1), (SEND, 1, 4, 6, 5), (SEND, 0, 2, 9, 6), (SEND, 1, 0, 5, 6), (READY, 2), (PAIRS, 2, (0, 1)),
    (ARRIVE, 1, 7, 0), (ARRIVE, 0, 9, 1), (ARRIVE, 1, 6, 3), (ARRIVE, 0, 5, 4), (ARRIVE, 0, 4, 6), (ARRIVE, 1, 3, 6),
    (SEND, 0, 9, 8, 0), (SEND, 0, 6, 11, 2), (SEND, 1, 3, 10, 2), (SEND, 0, 4, 6, 5), (READY, 3), (READY, 4),
    (ARRIVE, 0, 10, 0), (ARRIVE, 1, 11, 0), (ARRIVE, 1, 7, 1), (ARRIVE, 0, 6, 3), (ARRIVE, 1, 9, 4),
    (ARRIVE, 0, 5, 5), (SEND, 1, 7, 8, 1), (SEND, 0, 5, 7, 5), (BEGIN, 9), (SEND, 0, 3, 10, 2), (SEND, 1, 6, 11, 2),
    (SEND, 0, 2, 7, 4), (SEND, 0, 4, 6, 6), (PAIRS, 4, (0, 1, 2)), (ARRIVE, 0, 11, 0), (ARRIVE, 1, 10, 0),
    (ARRIVE, 0, 7, 2), (ARRIVE, 1, 8, 2), (ARRIVE, 1, 6, 4), (ARRIVE, 1, 5, 5), (SEND, 0, 7, 8, 2),
    (SEND, 1, 8, 9, 2), (BEGIN, 7), (SEND, 0, 3, 10, 3), (SEND, 1, 6, 11, 3), (SEND, 1, 2, 7, 4), (SEND, 1, 2, 9, 6),
    (SEND, 1, 4, 6, 6), (ARRIVE, 0, 10, 1), (ARRIVE, 1, 11, 1), (ARRIVE, 1, 7, 3), (ARRIVE, 0, 6, 4),
    (ARRIVE, 1, 9, 5), (ARRIVE, 0, 5, 6), (SEND, 0, 5, 7, 6), (SEND, 0, 6, 11, 3), (SEND, 1, 3, 10, 3),
    (SEND, 1, 2, 7, 5), (PAIRS, 3, (2, 4)), (ARRIVE, 1, 8, 0), (ARRIVE, 0, 11, 1), (ARRIVE, 1, 10, 1),
    (ARRIVE, 1, 6, 5), (ARRIVE, 0, 9, 6), (ARRIVE, 1, 5, 6), (SEND, 1, 5, 7, 6), (SEND, 0, 9, 8, 3),
    (SEND, 0, 3, 10, 4), (SEND, 1, 6, 11, 4), (READY, 5), (ARRIVE, 0, 8, 0), (ARRIVE, 1, 8, 1), (ARRIVE, 0, 11, 2),
    (ARRIVE, 1, 10, 2), (ARRIVE, 0, 7, 5), (ARRIVE, 0, 6, 5), (SEND, 0, 8, 7, 0), (SEND, 0, 7, 8, 5), (BEGIN, 10),
    (BEGIN, 11), (SEND, 1, 9, 8, 3), (SEND, 0, 6, 11, 4), (SEND, 1, 3, 10, 4), (PAIRS, 5, (1, 3, 4)),
    (ARRIVE, 0, 10, 2), (ARRIVE, 0, 8, 2), (ARRIVE, 1, 9, 2), (ARRIVE, 1, 11, 2), (ARRIVE, 0, 7, 4),
    (ARRIVE, 0, 6, 6), (SEND, 0, 8, 9, 2), (SEND, 0, 7, 8, 4), (BEGIN, 8), (SEND, 1, 9, 8, 4), (SEND, 0, 3, 10, 5),
    (SEND, 1, 6, 11, 5), (ARRIVE, 0, 10, 3), (ARRIVE, 1, 11, 3), (ARRIVE, 1, 7, 4), (ARRIVE, 0, 7, 6),
    (ARRIVE, 1, 9, 6), (ARRIVE, 1, 6, 6), (SEND, 0, 7, 8, 6), (SEND, 0, 6, 11, 5), (SEND, 1, 3, 10, 5),
    (SEND, 1, 9, 8, 6), (READY, 6), (ARRIVE, 0, 11, 3), (ARRIVE, 1, 10, 3), (ARRIVE, 1, 7, 5), (ARRIVE, 1, 7, 6),
    (SEND, 1, 7, 8, 5), (SEND, 0, 3, 10, 6), (SEND, 1, 6, 11, 6), (PAIRS, 6, (0, 2, 5)), (FOLD, (5,)),
    (ARRIVE, 0, 7, 0), (ARRIVE, 0, 8, 5), (SEND, 0, 8, 9, 5), (ARRIVE, 0, 8, 3), (ARRIVE, 0, 10, 4),
    (ARRIVE, 1, 11, 4), (SEND, 0, 6, 11, 6), (SEND, 1, 3, 10, 6), (READY, 7), (ARRIVE, 0, 9, 2), (ARRIVE, 0, 8, 4),
    (SEND, 0, 8, 9, 4), (ARRIVE, 1, 8, 3), (ARRIVE, 0, 11, 4), (ARRIVE, 1, 10, 4), (PAIRS, 7, (1, 3, 4)),
    (ARRIVE, 0, 8, 6), (ARRIVE, 1, 8, 4), (ARRIVE, 0, 10, 5), (ARRIVE, 1, 11, 5), (PAIRS, 7, (6,)),
    (ARRIVE, 1, 8, 5), (ARRIVE, 0, 11, 5), (ARRIVE, 1, 10, 5), (ARRIVE, 1, 8, 6), (SHARED, 7, (0,), 2),
    (ARRIVE, 0, 9, 5), (SHARED, 6, (3,), 0), (READY, 8), (ARRIVE, 0, 10, 6), (ARRIVE, 1, 11, 6), (PAIRS, 8, (3,)),
    (ARRIVE, 0, 9, 4), (SHARED, 8, (1,), 1), (ARRIVE, 0, 11, 6), (ARRIVE, 1, 10, 6), (READY, 9),
    (PAIRS, 9, (1, 3, 6)), (FOLD, (1, 3, 6)), (READY, 10), (READY, 11), (PAIRS, 11, (2, 8, 9)), (FOLD, (8,)),
    (PAIRS, 10, (2, 4, 9)), (FOLD, (2, 4, 9)), (SHARED, 11, (10,), 1), (SHARED, 11, (7,), 0), (FOLD, (11,)),
    (SHARED, 10, (7,), 0), (FOLD, (7,)), (SHARED, 10, (0,), 0), (FOLD, (0, 10)),
)

ROWS = 448
WINDOW = 128
CLUSTERS = 8
NONE = 1 << 20


def place():
    row, grp = lax.axis_index("row"), lax.axis_index("grp")
    return grp // 4, row // 2, grp % 4, row % 2


def device(x, y, z, core):
    return (lax.rem(y + 4, 4) * 2 + core, lax.rem(x + 4, 4) * 4 + lax.rem(z + 4, 4))


def scores(left, right):
    return lax.dot_general(
        left, right, (((1,), (1,)), ((), ())), preferred_element_type=jnp.float32
    )


def kernel(emb, scales, cid, rank, out, *refs):
    own, sib = refs[:SLOTS], refs[SLOTS : 2 * SLOTS]
    (
        unit, table, meta_own, meta_sib, first_own, first_sib, col, row_best, col_best, outgoing, incoming,
        recv, recv_meta, sib_recv, sib_recv_meta, sent, sent_meta, sib_sent, sib_sent_meta, local, back_sent, back_recv,
    ) = refs[2 * SLOTS :]
    x, y, z, core = place()
    root = ROOTS[0] + core * (ROOTS[1] - ROOTS[0])
    chunk_rows = ROWS // CHUNKS
    def other():
        return device(x, y, z, 1 - core)

    barrier = pltpu.get_barrier_semaphore()
    for dx, dy, dz in ((1, 0, 0), (-1, 0, 0), (0, 1, 0), (0, -1, 0), (0, 0, 1), (0, 0, -1)):
        pl.semaphore_signal(
            barrier, inc=1, device_id=device(x + dx, y + dy, z + dz, core), device_id_type=MESH
        )
    pl.semaphore_signal(barrier, inc=1, device_id=other(), device_id_type=MESH)

    def clear(i, _):
        row_best[i] = jnp.full((2 * WINDOW, WINDOW), -1.0, jnp.float32)
        col_best[i] = jnp.full((8, 2 * WINDOW), -1.0, jnp.float32)
        return 0

    lax.fori_loop(0, SLOTS * 4, clear, 0)

    factor = scales[...].T
    total = jnp.zeros((ROWS, 1), jnp.float32)
    for b in range(8):
        part = emb[:, b * 128 : (b + 1) * 128].astype(jnp.float32) * factor[:, b : b + 1]
        total = total + jnp.sum(part * part, axis=1, keepdims=True)
    inverse = lax.rsqrt(total + 1e-06)
    for b in range(8):
        part = emb[:, b * 128 : (b + 1) * 128].astype(jnp.float32) * factor[:, b : b + 1]
        unit[:, b * 128 : (b + 1) * 128] = (part * inverse).astype(jnp.bfloat16)

    cids, ranks = cid[...], rank[...]
    sub16 = lax.broadcasted_iota(jnp.int32, (16, ROWS), 0)
    member = sub16 == cids
    earlier = (
        lax.broadcasted_iota(jnp.int32, (ROWS, ROWS), 0) < lax.broadcasted_iota(jnp.int32, (ROWS, ROWS), 1)
    )
    before = jnp.dot(
        jnp.where(member, 1.0, 0.0).astype(jnp.bfloat16),
        jnp.where(earlier, 1.0, 0.0).astype(jnp.bfloat16),
        preferred_element_type=jnp.float32,
    )
    sub128 = lax.broadcasted_iota(jnp.int32, (WINDOW, ROWS), 0)
    start = jnp.sum(jnp.where(cids < sub128, 1, 0), axis=1, keepdims=True)
    position = jnp.sum(
        jnp.where(member, before + start[0:16].astype(jnp.float32), 0.0), axis=0, keepdims=True
    ).astype(jnp.int32)
    tile_start = jnp.minimum(start >> 4, (ROWS - WINDOW) // 16)
    window_start = tile_start * 16
    diagonal = lax.broadcasted_iota(jnp.int32, (WINDOW, WINDOW), 0) == lax.broadcasted_iota(
        jnp.int32, (WINDOW, WINDOW), 1
    )
    start_row = jnp.sum(jnp.where(diagonal, tile_start, 0), axis=0, keepdims=True)
    def make_table():
        for c in range(CLUSTERS):
            spot = window_start[c : c + 1, :] + lax.broadcasted_iota(jnp.int32, (WINDOW, ROWS), 0)
            hit = jnp.logical_and(spot == position, cids == c)
            table[c * WINDOW : (c + 1) * WINDOW, :] = jnp.where(hit, 1.0, 0.0).astype(jnp.bfloat16)
        digits = jnp.where(
            sub16 == 0, ranks >> 7, jnp.where(sub16 == 1, ranks & 127, jnp.where(sub16 == 2, 1, 0))
        ).astype(jnp.float32).astype(jnp.bfloat16)
        placed = scores(digits, table[...])
        slot_rank = jnp.where(placed[2:3] > 0.5, placed[0:1] * 128.0 + placed[1:2], float(NONE)).astype(jnp.int32)
        meta_own[root] = jnp.concatenate(
            [slot_rank[:, c * WINDOW : (c + 1) * WINDOW] for c in range(CLUSTERS)]
            + [start_row, jnp.zeros((7, WINDOW), jnp.int32)],
            axis=0,
        )

    def sort_chunk(k):
        spot = lax.broadcasted_iota(jnp.int32, (chunk_rows, ROWS), 0) + k * chunk_rows
        move = jnp.where(spot == position, 1.0, 0.0).astype(jnp.bfloat16)
        rows = jnp.dot(move, unit[...], preferred_element_type=jnp.float32).astype(jnp.bfloat16)
        for c in (0, 1):

            @pl.when(core == c)
            def _():
                own[ROOTS[c]][k * chunk_rows : (k + 1) * chunk_rows, :] = rows

    def piece(ref, chunk):
        return ref.at[pl.ds(chunk * chunk_rows, chunk_rows)]

    def to_sibling(slot, chunk):
        return pltpu.make_async_remote_copy(
            src_ref=own[slot] if chunk is None else piece(own[slot], chunk),
            dst_ref=sib[slot] if chunk is None else piece(sib[slot], chunk),
            send_sem=sib_sent.at[slot], recv_sem=sib_recv.at[slot],
            device_id=other(), device_id_type=MESH,
        )

    def meta_to_sibling(slot):
        return pltpu.make_async_remote_copy(
            src_ref=meta_own.at[slot], dst_ref=meta_sib.at[slot],
            send_sem=sib_sent_meta.at[slot], recv_sem=sib_recv_meta.at[slot],
            device_id=other(), device_id_type=MESH,
        )

    def target(e, d):
        ux, uy, uz = (q - p for p, q in zip(OFFSETS[e], OFFSETS[d]))
        return device(x - ux, y - uy, z - uz, core)

    def along(e, d, chunk):
        return pltpu.make_async_remote_copy(
            src_ref=own[e] if chunk is None else piece(own[e], chunk),
            dst_ref=own[d] if chunk is None else piece(own[d], chunk),
            send_sem=sent.at[d],
            recv_sem=recv.at[d * CHUNKS + (chunk or 0)],
            device_id=target(e, d), device_id_type=MESH,
        )

    def meta_along(e, d):
        return pltpu.make_async_remote_copy(
            src_ref=meta_own.at[e], dst_ref=meta_own.at[d],
            send_sem=sent_meta.at[d], recv_sem=recv_meta.at[d],
            device_id=target(e, d), device_id_type=MESH,
        )

    def starts_to_scalars(slot):
        return [
            pltpu.make_async_copy(meta.at[slot, pl.ds(8, 1)], first.at[slot], local.at[slot * 2 + n])
            for n, (meta, first) in enumerate(((meta_own, first_own), (meta_sib, first_sib)))
        ]

    def arrive(c, slot, chunk):
        if slot != ROOTS[c]:
            e = parent_of[(c, slot, chunk)]
            along(e, slot, chunk).wait_recv()
            if chunk == EXTRA:
                meta_along(e, slot).wait_recv()
        if chunk == EXTRA:
            meta_to_sibling(slot).start()
        to_sibling(slot, chunk).start()

    def send(c, e, d, chunk):
        if chunk == EXTRA:
            meta_along(e, d).start()
        along(e, d, chunk).start()

    parent_of = {}
    for item in PLAN:
        if item[0] == SEND:
            _, c, e, d, chunk = item
            parent_of[(c, d, chunk)] = e

    def begin(slot):
        meta_to_sibling(slot).wait_recv()
        for copy in starts_to_scalars(slot):
            copy.start()
        for n, meta in enumerate((meta_own, meta_sib)):
            tile = meta[slot, 0:8, :]
            mine = jnp.where(core == 0, tile, jnp.concatenate([tile[4:8], tile[0:4]], axis=0))
            turned = mine.astype(jnp.float32).T
            for q in range(4):
                col[slot * 4 + q, pl.ds(n * WINDOW, WINDOW), :] = jnp.broadcast_to(
                    turned[:, q : q + 1], (WINDOW, WINDOW)
                )

    def ready(slot):
        to_sibling(slot, None).wait_recv()
        for copy in starts_to_scalars(slot):
            copy.wait()

    def window(slot, cluster):
        return [
            ref[pl.ds(first[slot, 0, cluster] * 16, WINDOW), :]
            for ref, first in ((own[slot], first_own), (sib[slot], first_sib))
        ]

    def pairs(b, group, count, base, itself=False):
        def one(i, _):
            q = base + i
            cluster = core * 4 + q
            right = jnp.concatenate(window(b, cluster), axis=0)
            left = jnp.concatenate([w for a in group for w in window(a, cluster)], axis=0)
            found = scores(left, right)
            right_rank = jnp.concatenate(
                [meta[b, pl.ds(cluster, 1), :] for meta in (meta_own, meta_sib)], axis=1
            ).astype(jnp.float32)
            for n, a in enumerate(group):
                value = found[n * 2 * WINDOW : (n + 1) * 2 * WINDOW]
                less = right_rank < jnp.concatenate([col[a * 4 + q]] * 2, axis=1)
                to_left = jnp.where(less, value, -1.0)
                row_best[a * 4 + q] = jnp.maximum(
                    row_best[a * 4 + q], jnp.maximum(to_left[:, :WINDOW], to_left[:, WINDOW:])
                )
                if not itself:
                    to_right = jnp.where(less, -1.0, value).reshape(2 * WINDOW // 8, 8, 2 * WINDOW)
                    col_best[b * 4 + q] = jnp.maximum(col_best[b * 4 + q], jnp.max(to_right, axis=0))
            return 0

        lax.fori_loop(0, count, one, 0, unroll=4)

    def on_core(c, steps):
        @pl.when(core == c)
        def _():
            for step in steps:
                step()

    def sent_to(d):
        along((d + 1) % SLOTS, d, None).wait_send()
        meta_along((d + 1) % SLOTS, d).wait_send()

    def reply(d, n):
        away = [[q - p for p, q in zip(OFFSETS[ROOTS[c]], OFFSETS[d])] for c in (n, 1 - n)]
        ox, oy, oz = (first + core * (second - first) for first, second in zip(*away))
        return pltpu.make_async_remote_copy(
            src_ref=outgoing.at[n * SLOTS + d], dst_ref=incoming.at[n * SLOTS + d],
            send_sem=back_sent.at[d * 2 + n], recv_sem=back_recv.at[d * 2 + n],
            device_id=device(x + ox, y + oy, z + oz, core if n == 0 else 1 - core), device_id_type=MESH,
        )

    def replies(d, what):
        if d not in ROOTS:
            getattr(reply(d, 0), what)()
        elif ROOTS[0] != ROOTS[1]:
            on_core(1 - ROOTS.index(d), [getattr(reply(d, 0), what)])
        getattr(reply(d, 1), what)()

    lane = lax.broadcasted_iota(jnp.int32, (2 * WINDOW, WINDOW), 1)

    def fold(group):
        best = jnp.full((2 * WINDOW, WINDOW), -1.0, jnp.float32)
        for n, d in enumerate(group):
            for q in range(4):
                best = jnp.where(lane == n * 8 + q, jnp.max(row_best[d * 4 + q], axis=1, keepdims=True), best)
        turned = best.T
        for n, d in enumerate(group):
            rows = jnp.concatenate(
                [jnp.max(col_best[d * 4 + q], axis=0, keepdims=True) for q in range(4)]
                + [jnp.full((4, 2 * WINDOW), -1.0, jnp.float32)],
                axis=0,
            )
            rows = jnp.maximum(rows, turned[n * 8 : (n + 1) * 8])
            for half in (0, 1):
                outgoing[half * SLOTS + d] = rows[:, half * WINDOW : (half + 1) * WINDOW]
            replies(d, "start")

    pending = [[], []]

    def flush():
        for c in (0, 1):
            if pending[c]:
                on_core(c, pending[c])
            pending[c] = []

    pl.semaphore_wait(barrier, 7)
    for item in PLAN:
        if item[0] == ARRIVE:
            pending[item[1]].append(functools.partial(arrive, *item[1:]))
            continue
        if item[0] == SEND:
            pending[item[1]].append(functools.partial(send, *item[1:]))
            continue
        flush()
        if item[0] == SORT:
            sort_chunk(item[1])
        elif item[0] == TABLE:
            make_table()
        elif item[0] == BEGIN:
            begin(item[1])
        elif item[0] == READY:
            ready(item[1])
        elif item[0] == PAIRS:
            pairs(item[1], item[2], 4, 0)
        elif item[0] == SHARED:
            pairs(item[1], item[2], 2, (x, y, z)[item[3]] // 2 * 2)
        elif item[0] == FOLD:
            fold(item[1])
        else:
            pairs(item[1], (item[1],), 4, 0, itself=True)
    flush()

    for d in range(SLOTS):
        to_sibling(d, None).wait_send()
        meta_to_sibling(d).wait_send()
        if d not in ROOTS:
            sent_to(d)
        elif ROOTS[0] != ROOTS[1]:
            on_core(1 - ROOTS.index(d), [functools.partial(sent_to, d)])
    for what in ("wait_send", "wait_recv"):
        for d in range(SLOTS):
            replies(d, what)
    incoming[root] = outgoing[root]
    final = []
    for n in (0, 1):
        best = incoming[n * SLOTS]
        for d in range(1, SLOTS):
            best = jnp.maximum(best, incoming[n * SLOTS + d])
        final.append(best)
    lower = jnp.where(core == 0, final[0], final[1])
    upper = jnp.where(core == 0, final[1], final[0])
    line = jnp.concatenate([lower[q : q + 1] for q in range(4)] + [upper[q : q + 1] for q in range(4)], axis=1)
    high = line.astype(jnp.bfloat16)
    rest = line - high.astype(jnp.float32)
    middle = rest.astype(jnp.bfloat16)
    low = (rest - middle.astype(jnp.float32)).astype(jnp.bfloat16)
    sub = lax.broadcasted_iota(jnp.int32, (16, CLUSTERS * WINDOW), 0)
    parts = jnp.where(
        sub == 0, high.astype(jnp.float32),
        jnp.where(sub == 1, middle.astype(jnp.float32), jnp.where(sub == 2, low.astype(jnp.float32), 0.0)),
    ).astype(jnp.bfloat16)
    out[...] = jnp.sum(jnp.dot(parts, table[...], preferred_element_type=jnp.float32), axis=0, keepdims=True)


def local(embeddings, scales, cluster_id, doc_rank):
    vmem = pl.BlockSpec(memory_space=pltpu.VMEM)
    dma = pltpu.SemaphoreType.DMA
    best = pl.pallas_call(
        kernel,
        out_shape=jax.ShapeDtypeStruct((1, ROWS), jnp.float32),
        in_specs=[vmem] * 4,
        out_specs=vmem,
        scratch_shapes=[pltpu.VMEM((ROWS, 1024), jnp.bfloat16)] * (2 * SLOTS)
        + [
            pltpu.VMEM((ROWS, 1024), jnp.bfloat16),
            pltpu.VMEM((CLUSTERS * WINDOW, ROWS), jnp.bfloat16),
            pltpu.VMEM((SLOTS, 16, WINDOW), jnp.int32),
            pltpu.VMEM((SLOTS, 16, WINDOW), jnp.int32),
            pltpu.SMEM((SLOTS, 1, WINDOW), jnp.int32),
            pltpu.SMEM((SLOTS, 1, WINDOW), jnp.int32),
            pltpu.VMEM((SLOTS * 4, 2 * WINDOW, WINDOW), jnp.float32),
            pltpu.VMEM((SLOTS * 4, 2 * WINDOW, WINDOW), jnp.float32),
            pltpu.VMEM((SLOTS * 4, 8, 2 * WINDOW), jnp.float32),
            pltpu.VMEM((2 * SLOTS, 8, WINDOW), jnp.float32),
            pltpu.VMEM((2 * SLOTS, 8, WINDOW), jnp.float32),
            dma((SLOTS * CHUNKS,)),
            dma((SLOTS,)),
            dma((SLOTS,)),
            dma((SLOTS,)),
            dma((SLOTS,)),
            dma((SLOTS,)),
            dma((SLOTS,)),
            dma((SLOTS,)),
            dma((2 * SLOTS,)),
            dma((2 * SLOTS,)),
            dma((2 * SLOTS,)),
        ],
        compiler_params=pltpu.CompilerParams(
            collective_id=0, has_side_effects=True, vmem_limit_bytes=56 * 2**20
        ),
        cost_estimate=pl.CostEstimate(flops=30 * 10**9, bytes_accessed=2**20, transcendentals=0),
        name="nearest_in_cluster",
    )(embeddings, scales.T, cluster_id.reshape(1, ROWS), doc_rank.reshape(1, ROWS))
    return best.reshape(ROWS)


def solution(mesh):
    return jax.shard_map(
        local,
        mesh=mesh,
        in_specs=(P(("row", "grp"), None), P(("row", "grp"), None), P(("row", "grp")), P(("row", "grp"))),
        out_specs=P(("row", "grp")),
        check_vma=False,
    )
```
